768 devices in a mesh: slab: 12 (over z), sub: 64 (over x, y, core).
Axes of the slice: x: 4, y: 8, z: 12, core: 2. Of those that a mesh axis runs over, the one named last changes fastest.
Arguments:
- fields: float32 [5, 512, 768, 128], P(None, None, ('slab', 'sub')), may hold values from -6 to 6
- metric: float32 [3, 768, 128], P(None, ('slab', 'sub')), may hold values from 0.5 to 2
- diffusivity: float32 [5], replicated, may hold values from 0.0001 to 0.001
- joule_heat: float32 [512, 768, 128], P(None, ('slab', 'sub')), may hold values from 0.5 to 5
- face_flip: int32 [768], P(('slab', 'sub')), may hold values from 0 to 1
- coarse_decay: float32 [8, 768, 128], P(None, ('slab', 'sub')), may hold values from 0 to 1
Outputs:
- advanced: float32 [5, 512, 768, 128], P(None, None, ('slab', 'sub'))
- pressure: float32 [512, 768, 128], P(None, ('slab', 'sub'))
The draws below stay inside these ranges and needn't reach their ends.
All inputs are finite; a program needn't handle non-finite values.
Results may differ from the reference program's by a relative error of at most 0.0002.
Values sent between devices are 32-bit elements; how exact they have to be, the bound alone decides.
A program may use at most 32 MiB of HBM per device.

```python
import math
import jax
import jax.numpy as jnp
import numpy as np
from jax import lax

NODES = 512
FIELDS = 5
VERTEX_MODES = 8
LATERAL_ELEMENTS = 128
GAP_POSITIONS = 768
N_SLAB = 12
N_SUB = 64


def draw_coarse_decay(key, part):
    mode_key, keep_key, device_key, place_key, cutoff_key, quick_key, rough_key = jax.random.split(key, 7)
    slow_share = 0.5
    is_slow = jax.random.uniform(mode_key, (VERTEX_MODES, 1, LATERAL_ELEMENTS)) < slow_share
    keep_share = jax.random.uniform(keep_key, (VERTEX_MODES, 1, LATERAL_ELEMENTS), minval=0.1, maxval=0.45)
    device_factor = jnp.exp(jax.random.uniform(device_key, (1, GAP_POSITIONS, 1), minval=-0.7, maxval=0.0))
    roughness = jnp.exp(jax.random.uniform(rough_key, (VERTEX_MODES, GAP_POSITIONS, LATERAL_ELEMENTS), minval=-0.7, maxval=0.7))
    slow_log = jnp.log(0.1) * keep_share * device_factor * roughness / GAP_POSITIONS
    memory_len = jnp.exp(jax.random.uniform(quick_key, (VERTEX_MODES, 1, LATERAL_ELEMENTS), minval=jnp.log(30.0), maxval=jnp.log(50.0)))
    fast_log = -device_factor * roughness / memory_len
    logarithm_rate = jnp.where(is_slow, slow_log, fast_log)
    pulse_onset = jax.random.randint(place_key, (3, VERTEX_MODES, 1, LATERAL_ELEMENTS), 0, GAP_POSITIONS)
    position_grid = jnp.arange(GAP_POSITIONS)[None, None, :, None]
    inside_pulse = jnp.any(position_grid == pulse_onset, axis=0)
    pulse_cutoff = jax.random.uniform(cutoff_key, (VERTEX_MODES, 1, LATERAL_ELEMENTS), minval=0.65, maxval=0.85)
    damping_rate = jnp.exp(logarithm_rate) * jnp.where(inside_pulse, pulse_cutoff, 1.0)
    return damping_rate.astype(jnp.float32)


def place_ends(drawn, own_key, low, largest):
    spot = [jax.random.randint(jax.random.fold_in(own_key, axis), (), 0, length) for axis, length in enumerate(drawn.shape)]
    main_axis = drawn.shape.index(max(drawn.shape))
    next_to = spot[:main_axis] + [(spot[main_axis] + 1) % drawn.shape[main_axis]] + spot[main_axis + 1:]
    return drawn.at[tuple(spot)].set(low).at[tuple(next_to)].set(largest)


def levels(key, shape, cuts, least, top_value):
    gain, own = 1.0, jax.random.fold_in(key, 6)
    for dim, shards_of in cuts:
        steps = jnp.exp(jax.random.uniform(jax.random.fold_in(own, dim), (shards_of,), jnp.float32, least / len(cuts), top_value / len(cuts)))
        gain = gain * jnp.repeat(steps, shape[dim] // shards_of).reshape([-1 if axis == dim else 1 for axis in range(len(shape))])
    return gain


def normal_values(stream_key, shape, width, most, shards=(), dtype=jnp.bfloat16):
    values = jax.random.normal(stream_key, shape, jnp.float32) * width
    if len(shards) > 0:
        values = levels(stream_key, shape, shards, -0.22, 0.18) * values
    return jnp.clip(values, min=-most, max=most).astype(dtype)


def setup_inputs(seed: int = 0) -> dict:
    seeds = jax.random.split(jax.random.key(seed), 7)
    return {
        "fields": normal_values(seeds[0], (FIELDS, NODES, GAP_POSITIONS, LATERAL_ELEMENTS), 1.0, 6.0, ((2, 768),), jnp.float32),
        "metric": jnp.clip(jnp.exp(math.log(2.0) - 1.3862944 * jax.random.uniform(seeds[1], (3, GAP_POSITIONS, LATERAL_ELEMENTS), jnp.float32) ** levels(seeds[1], (3, GAP_POSITIONS, LATERAL_ELEMENTS), ((1, 768),), -0.2, 0.2)), 0.5, 2.0),
        "diffusivity": jnp.clip(jnp.exp(jax.random.uniform(seeds[2], (FIELDS,), jnp.float32, math.log(0.0001), math.log(0.001))), 0.0001, 0.001),
        "joule_heat": jnp.clip(jnp.exp(math.log(5.0) - 2.3025851 * jax.random.uniform(seeds[3], (NODES, GAP_POSITIONS, LATERAL_ELEMENTS), jnp.float32) ** levels(seeds[3], (NODES, GAP_POSITIONS, LATERAL_ELEMENTS), ((1, 768),), -0.2, 0.2)), 0.5, 5.0),
        "face_flip": place_ends(jax.random.randint(seeds[4], (GAP_POSITIONS,), 0, 2), jax.random.fold_in(seeds[4], 1), 0, 1).astype(jnp.int32),
        "coarse_decay": draw_coarse_decay(jax.random.fold_in(seeds[6], 71), 0),
    }


HIGHEST = lax.Precision.HIGHEST
FORMS = ('ia,fajkcl->fijkcl', 'ja,fiakcl->fijkcl', 'ka,fijacl->fijkcl')

def spectral_tables():
    points = np.cos(np.pi * np.arange(8) / 7.0)
    endings = np.ones(8)
    endings[0] = 2.0
    endings[7] = 2.0
    weighted = endings * (-1.0) ** np.arange(8)
    quotient = weighted[:, None] / weighted[None, :]
    spacing = points[:, None] - points[None, :] + np.eye(8)
    derive = quotient / spacing
    derive = derive - np.eye(8) * np.sum(derive, axis=1)[:, None]
    column_sq = np.sum(derive * derive, axis=0)
    index_all = np.arange(512)
    digits = (index_all // 64, index_all // 8 % 8, index_all % 8)
    diagonal = np.stack([column_sq[digit_set] for digit_set in digits])
    halves = np.stack([(1.0 - points) / 2.0, (1.0 + points) / 2.0])
    vertex = np.ones((8, 512))
    for corner in range(8):
        for position in range(3):
            vertex[corner] = vertex[corner] * halves[corner >> 2 - position & 1][digits[position]]
    return (jnp.asarray(derive, jnp.float32), jnp.asarray(diagonal, jnp.float32), jnp.asarray(vertex, jnp.float32))

def along(field, derive, direction):
    leading = field.shape[0]
    cube_view = field.reshape((leading, 8, 8, 8) + field.shape[2:])
    result = jnp.einsum(FORMS[direction], derive, cube_view, precision=HIGHEST)
    return result.reshape(field.shape)

def advance(fields, metric, diffusivity, joule_heat, derive):
    scales = [metric[direction][None, None] for direction in range(3)]
    slopes = [scales[direction] * along(fields, derive, direction) for direction in range(3)]
    carried = fields[0:1] * slopes[0] + fields[1:2] * slopes[1] + fields[2:3] * slopes[2]
    spread = -(scales[0] * along(slopes[0], derive.T, 0) + scales[1] * along(slopes[1], derive.T, 1) + scales[2] * along(slopes[2], derive.T, 2))
    heat_in = joule_heat * (1.0 + 0.5 * jnp.tanh(fields[3])) * jax.nn.sigmoid(-fields[4])
    lifting = 0.3 * fields[3] - 0.5 * jax.nn.sigmoid(fields[4])
    nothing = jnp.zeros_like(heat_in)
    source = jnp.stack([nothing, lifting, nothing, heat_in, 0.2 * heat_in])
    stepped = fields - 0.01 * carried + diffusivity[:, None, None, None] * spread + 0.05 * source
    node_k = jnp.arange(512) % 8
    inside = ((node_k > 0) & (node_k < 7)).astype(jnp.float32)
    keeper = jnp.stack([inside, inside, inside, jnp.ones_like(inside), jnp.ones_like(inside)])
    return stepped * keeper[:, :, None, None]

def divergence(velocity, metric, derive):
    summed = metric[0][None, None] * along(velocity[0:1], derive, 0)
    summed = summed + metric[1][None, None] * along(velocity[1:2], derive, 1)
    summed = summed + metric[2][None, None] * along(velocity[2:3], derive, 2)
    return summed

def pressure_pair(source, metric, derive, diagonal):
    denominator = 1.0
    for direction in range(3):
        denominator = denominator + metric[direction][None, None] ** 2 * diagonal[direction][None, :, None, None]
    weight = 0.5 / denominator
    first_guess = weight * source
    applied = first_guess
    for direction in range(3):
        scale_now = metric[direction][None, None]
        applied = applied + scale_now * along(scale_now * along(first_guess, derive, direction), derive.T, direction)
    return jnp.concatenate([first_guess, source - applied], axis=0)

def join_lateral(field):
    cube_view = field.reshape((field.shape[0], 8, 8, 8) + field.shape[2:])
    lower_face = cube_view[:, :, 0]
    upper_face = cube_view[:, :, 7]
    shared = 0.5 * (lower_face + jnp.roll(upper_face, 1, axis=-1))
    joined = jnp.concatenate([shared[:, :, None], cube_view[:, :, 1:7], jnp.roll(shared, -1, axis=-1)[:, :, None]], axis=2)
    return joined.reshape(field.shape)

def oriented(face, flipped):
    face_grid = face.reshape((face.shape[0], 8, 8) + face.shape[2:])
    turned = face_grid[:, :, ::-1].reshape(face.shape)
    return jnp.where(flipped, turned, face)

def join_chain(field, face_flip):
    first_face = field[:, :64]
    last_face = field[:, 448:]
    flipped = (face_flip == 1)[:, None]
    chain_len = field.shape[2]
    position = jnp.arange(chain_len)[:, None]
    from_left = jnp.concatenate([jnp.zeros_like(last_face[:, :, :1]), last_face[:, :, :-1]], axis=2)
    from_right = jnp.concatenate([oriented(first_face, flipped)[:, :, 1:], jnp.zeros_like(first_face[:, :, :1])], axis=2)
    new_first = jnp.where(position == 0, first_face, 0.5 * (first_face + oriented(from_left, flipped)))
    new_last = jnp.where(position == chain_len - 1, last_face, 0.5 * (last_face + from_right))
    return jnp.concatenate([new_first, field[:, 64:448], new_last], axis=1)

def by_slab(worker, arrays):

    def split_slab(member):
        shaped = member.reshape(member.shape[:-2] + (N_SLAB, N_SUB, member.shape[-1]))
        return jnp.moveaxis(shaped, -3, 0)
    result = lax.map(lambda pieces: worker(*pieces), tuple((split_slab(member) for member in arrays)))
    joined = jnp.moveaxis(result, 0, -3)
    return joined.reshape(joined.shape[:-3] + (N_SLAB * N_SUB, joined.shape[-1]))

def coarse_solve(coarse_rhs, coarse_decay):
    gain_root = jnp.sqrt((1.0 - coarse_decay) * (1.0 + coarse_decay))
    rates = jnp.moveaxis(coarse_decay, 1, 0)

    def chain_step(carry_state, inputs):
        rate_now, push_now = inputs
        carry_state = rate_now * carry_state + push_now
        return (carry_state, carry_state)
    start_state = jnp.zeros_like(coarse_rhs[:, 0])
    final_state, forward = lax.scan(chain_step, start_state, (rates, jnp.moveaxis(gain_root * coarse_rhs, 1, 0)))
    final_back, backward = lax.scan(chain_step, start_state, (rates, jnp.moveaxis(gain_root, 1, 0) * forward), reverse=True)
    return jnp.moveaxis(backward, 0, 1)

def reference(fields, metric, diffusivity, joule_heat, face_flip, coarse_decay):
    derive, diagonal, vertex = spectral_tables()

    def step_block(block_fields, block_metric, block_heat):
        return advance(block_fields, block_metric, diffusivity, block_heat, derive)
    stepped = by_slab(step_block, (fields, metric, joule_heat))
    advanced = join_chain(join_lateral(stepped), face_flip)

    def press_block(block_fields, block_metric):
        source = divergence(block_fields[0:3], block_metric, derive)
        return pressure_pair(source, block_metric, derive, diagonal)
    press_pair = by_slab(press_block, (advanced, metric))
    press_pair = join_chain(join_lateral(press_pair), face_flip)
    coarse_rhs = jnp.einsum('mn,ncl->mcl', vertex / 64.0, press_pair[1], precision=HIGHEST)
    backward = coarse_solve(coarse_rhs, coarse_decay)
    pressure = press_pair[0] + jnp.einsum('mn,mcl->ncl', vertex, backward, precision=HIGHEST)
    return (advanced, pressure)
```

```python
import functools

import jax
import jax.numpy as jnp
import numpy as np
from jax import lax
from jax.experimental import pallas as pl
from jax.experimental.pallas import tpu as pltpu
from jax.sharding import PartitionSpec as P

MESH = pl.DeviceIdType.MESH
F32 = jnp.float32

POINTS = np.cos(np.pi * np.arange(8) / 7.0)


def derivative():
    endings = np.ones(8)
    endings[0] = endings[7] = 2.0
    weighted = endings * (-1.0) ** np.arange(8)
    spacing = POINTS[:, None] - POINTS[None, :] + np.eye(8)
    derive = weighted[:, None] / weighted[None, :] / spacing
    return derive - np.eye(8) * np.sum(derive, axis=1)[:, None]


D = derivative()
K = D.T @ D
COLUMN_SQ = np.sum(D * D, axis=0)
H = np.stack([(1.0 - POINTS) / 2.0, (1.0 + POINTS) / 2.0])


def half_tables(matrix):
    even = (matrix[:4, :4] + matrix[:4, :3:-1]) / 2.0
    odd = (matrix[:4, :4] - matrix[:4, :3:-1]) / 2.0
    return even.tolist(), odd.tolist()


D_EVEN, D_ODD = half_tables(D)
K_EVEN, K_ODD = half_tables(K)


def dot4(row, parts):
    total = row[0] * parts[0]
    for a in range(1, 4):
        total = total + row[a] * parts[a]
    return total


def split(x):
    return [x[a] + x[7 - a] for a in range(4)], [x[a] - x[7 - a] for a in range(4)]


def apply_d(even, odd, p):
    from_even, from_odd = dot4(D_EVEN[p], even), dot4(D_ODD[p], odd)
    return from_odd + from_even, from_odd - from_even


def apply_k(even, odd, p):
    from_even, from_odd = dot4(K_EVEN[p], even), dot4(K_ODD[p], odd)
    return from_even + from_odd, from_even - from_odd


def ring(n, d):
    return min(d, n - d)


def kernel(
    sizes, fields, heat, metric, diffusivity, flip, decay, adv_out, prs_out,
    f, q, met, dif, flp, dec, s, u, tt, dv, fg, res, wgt, proj, kept,
    face_l, face_r, got_l, got_r, pface_l, pface_r, pgot_l, pgot_r,
    near_out, near, mine, partner, chips, stat, pre, slabs, zstat,
    load_sem, out_sem, face_send, face_recv, pface_send, pface_recv, near_send, near_recv,
    pair_sem, chip_sem, stat_sem, slab_sem, zstat_sem,
):
    nz, nx, ny = sizes
    chips_n = nx * ny
    sub_n = 2 * chips_n
    total = nz * sub_n
    z, sub = lax.axis_index("slab"), lax.axis_index("sub")
    core = lax.rem(sub, 2)
    chip = lax.div(sub, 2)
    cx, cy = lax.div(chip, ny), lax.rem(chip, ny)
    here = z * sub_n + sub
    at_start, at_end = here == 0, here == total - 1
    side = 2 * core - 1

    def at(position):
        position = lax.rem(position + total, total)
        return (lax.div(position, sub_n), lax.rem(position, sub_n))

    other_core = (z, sub - side)
    before, after = at(here - 1), at(here + 1)
    outer, outer_two, inner_two = at(here + side), at(here + 2 * side), at(here - 2 * side)
    chip_order = sorted(range(1, chips_n), key=lambda d: -(ring(nx, d // ny) + ring(ny, d % ny)))
    slab_order = sorted(range(1, nz), key=lambda d: -ring(nz, d))

    def chip_peer(d):
        px, py = lax.rem(cx + d // ny, nx), lax.rem(cy + d % ny, ny)
        return (z, (px * ny + py) * 2 + core)

    def slab_peer(d):
        return (lax.rem(z + d, nz), sub)

    def send(src, dst, send_sem, recv_sem, device):
        copy = pltpu.make_async_remote_copy(
            src_ref=src, dst_ref=dst, send_sem=send_sem, recv_sem=recv_sem,
            device_id=device, device_id_type=MESH,
        )
        copy.start()
        return copy

    def wait_bytes(ref, sem):
        pltpu.make_async_copy(ref, ref, sem).wait()

    loads = [
        pltpu.make_async_copy(decay, dec, load_sem.at[0]),
        pltpu.make_async_copy(metric, met, load_sem.at[1]),
        pltpu.make_async_copy(flip, flp, load_sem.at[2]),
        pltpu.make_async_copy(diffusivity, dif, load_sem.at[3]),
        pltpu.make_async_copy(fields, f, load_sem.at[4]),
        pltpu.make_async_copy(heat, q, load_sem.at[5]),
    ]
    for copy in loads:
        copy.start()

    barrier = pltpu.get_barrier_semaphore()
    targets = [other_core, outer, inner_two]
    targets += [chip_peer(d) for d in chip_order] + [slab_peer(d) for d in slab_order]
    for device in targets:
        pl.semaphore_signal(barrier, inc=1, device_id=device, device_id_type=MESH)

    for copy in loads:
        copy.wait()

    row = lax.broadcasted_iota(jnp.int32, (8, 128), 0)
    zero = jnp.zeros((8, 128), F32)
    wall = jnp.where((row == 0) | (row == 7), 0.0, 1.0)
    turned = (zero + flp[0].astype(F32)) == 1.0
    m = [jnp.broadcast_to(met[d], (8, 128)) for d in range(3)]
    msq = [m[d] * m[d] for d in range(3)]

    def by_row(values):
        out = zero + float(values[7])
        for k in range(7):
            out = jnp.where(row == k, float(values[k]), out)
        return out

    def reverse(x):
        half = pltpu.roll(x, 4, 0)
        pairs = jnp.where(lax.rem(row, 4) < 2, pltpu.roll(half, 6, 0), pltpu.roll(half, 2, 0))
        return jnp.where(lax.rem(row, 2) == 0, pltpu.roll(pairs, 7, 0), pltpu.roll(pairs, 1, 0))

    def oriented(x):
        return jnp.where(turned, reverse(x), x)

    def tile(ref, base):
        return ref.at[pl.ds(pl.multiple_of(base, 8), 8), :]

    def strided(ref, base, k):
        return ref[pl.ds(base + k, 8, stride=8), :]

    def start_plane(i):
        def line(j, carry):
            at_row = i * 64 + j * 8
            x = [tile(f, n * 512 + at_row)[...] for n in range(5)]
            warm = jnp.tanh(x[3])
            bubbles = jnp.tanh(0.5 * x[4])
            heating = tile(q, at_row)[...] * (0.05 + 0.025 * warm) * (0.5 - 0.5 * bubbles)
            lifting = 0.015 * x[3] - 0.0125 - 0.0125 * bubbles
            added = [x[0], x[1] + lifting, x[2], x[3] + heating, x[4] + 0.2 * heating]
            for n in range(5):
                tile(s, n * 512 + at_row)[...] = added[n]
            for n in range(3):
                tile(u, n * 512 + at_row)[...] = 0.01 * m[n] * x[n]
            return carry

        lax.fori_loop(0, 8, line, 0, unroll=2)

    def step_plane(n, i):
        at_row = i * 64
        base = n * 512 + at_row
        rate = dif[n]
        c1, c2 = rate * msq[1], rate * msq[2]
        even, odd = split([strided(f, base, k) for k in range(8)])
        for p in range(4):
            slopes, bends = apply_d(even, odd, p), apply_k(even, odd, p)
            for k, slope, bend in zip((p, 7 - p), slopes, bends):
                tt[8 * k : 8 * k + 8, :] = strided(u, 1024 + at_row, k) * slope + c2 * bend
        even, odd = split([tile(f, base + 8 * j)[...] for j in range(8)])
        for p in range(4):
            slopes, bends = apply_d(even, odd, p), apply_k(even, odd, p)
            for j, slope, bend in zip((p, 7 - p), slopes, bends):
                gone = tile(u, 512 + at_row + 8 * j)[...] * slope + c1 * bend
                gone = gone + strided(tt, 0, j)
                tile(s, base + 8 * j)[...] = tile(s, base + 8 * j)[...] - gone

    def step_lines(n, pairs):
        c0 = dif[n] * msq[0]
        keep = jnp.where(zero + (n < 3).astype(F32) > 0.5, wall, 1.0)

        def line(j, carry):
            base = n * 512 + j * 8
            even, odd = split([tile(f, base + 64 * i)[...] for i in range(8)])
            for p in pairs:
                slopes, bends = apply_d(even, odd, p), apply_k(even, odd, p)
                for i, slope, bend in zip((p, 7 - p), slopes, bends):
                    gone = tile(u, i * 64 + j * 8)[...] * slope + c0 * bend
                    tile(s, base + 64 * i)[...] = keep * (tile(s, base + 64 * i)[...] - gone)
            return carry

        lax.fori_loop(0, 8, line, 0, unroll=2)

    def join_span(ref, base):
        low, high = tile(ref, base), tile(ref, base + 56)
        shared = 0.5 * (low[...] + pltpu.roll(high[...], 1, 1))
        low[...] = shared
        high[...] = pltpu.roll(shared, 127, 1)

    def stage_faces(n):
        for j in range(8):
            spot = n * 64 + 8 * j
            tile(face_l, spot)[...] = oriented(tile(s, n * 512 + 8 * j)[...])
            tile(face_r, spot)[...] = tile(s, n * 512 + 448 + 8 * j)[...]

    def each(low, high, body):
        def run(n, carry):
            body(n)
            return carry

        lax.fori_loop(low, high, run, 0)

    near_out[0:8, :] = dec[...]
    near_out[8:16, :] = zero + flp[0].astype(F32)

    for i in (0, 7):
        start_plane(i)

    def velocity_faces(n):
        for i in (0, 7):
            step_plane(n, i)
        step_lines(n, (0,))
        for i in (0, 7):
            join_span(s, n * 512 + i * 64)
        stage_faces(n)

    each(0, 3, velocity_faces)

    pl.semaphore_wait(barrier, len(targets))
    faces = [
        send(face_l.at[0:192], got_r.at[0:192], face_send.at[0], face_recv.at[0], before),
        send(face_r.at[0:192], got_l.at[0:192], face_send.at[1], face_recv.at[1], after),
    ]
    nears = [
        send(near_out, near.at[0], near_send.at[0], near_recv.at[0], other_core),
        send(near_out, near.at[1], near_send.at[1], near_recv.at[1], outer),
        send(near_out, near.at[2], near_send.at[2], near_recv.at[2], outer_two),
    ]

    for p in (1, 2, 3):
        for i in (p, 7 - p):
            start_plane(i)

    def velocity_rest(n):
        def plane(i, carry):
            step_plane(n, i)
            return carry

        lax.fori_loop(1, 7, plane, 0)
        step_lines(n, (1, 2, 3))
        for i in range(1, 7):
            join_span(s, n * 512 + i * 64)

    each(0, 3, velocity_rest)

    def scalars(n):
        def plane(i, carry):
            step_plane(n, i)
            return carry

        lax.fori_loop(0, 8, plane, 0)
        step_lines(n, (0, 1, 2, 3))
        for i in range(8):
            join_span(s, n * 512 + i * 64)
        stage_faces(n)

    each(3, 5, scalars)
    faces += [
        send(face_l.at[192:320], got_r.at[192:320], face_send.at[2], face_recv.at[2], before),
        send(face_r.at[192:320], got_l.at[192:320], face_send.at[3], face_recv.at[3], after),
    ]

    across = msq[2] * by_row(COLUMN_SQ) + 1.0
    for a in range(4):
        for b in range(4):
            under = across + (float(COLUMN_SQ[a]) * msq[0] + float(COLUMN_SQ[b]) * msq[1])
            wgt[8 * (4 * a + b) : 8 * (4 * a + b) + 8, :] = 0.5 / under

    for copy in nears:
        copy.wait()
    own_a, partner_a, outer_a, far_a = dec[...], near[0, 0:8, :], near[1, 0:8, :], near[2, 0:8, :]
    first_core = zero + core.astype(F32) < 0.5
    not_start = 1.0 - at_start.astype(F32)
    not_end = 1.0 - at_end.astype(F32)
    a_0, a_1 = jnp.where(first_core, own_a, partner_a), jnp.where(first_core, partner_a, own_a)
    a_m, a_p = jnp.where(first_core, outer_a, far_a), jnp.where(first_core, far_a, outer_a)
    chip_first = (z * chips_n + chip == 0).astype(F32)
    chip_last = (z * chips_n + chip == nz * chips_n - 1).astype(F32)

    def root(a):
        return jnp.sqrt((1.0 - a) * (1.0 + a))

    s_0, s_1 = root(a_0), root(a_1)
    s_m, s_p = (1.0 - chip_first) * root(a_m), (1.0 - chip_last) * root(a_p)
    a_m, a_p = (1.0 - chip_first) * a_m, (1.0 - chip_last) * a_p
    ends_last = row < 4
    A_0, A_1 = jnp.where(ends_last, a_0, a_1), jnp.where(ends_last, a_1, a_p)
    R_0, R_1 = jnp.where(ends_last, a_m, a_0), jnp.where(ends_last, a_0, a_1)
    C_0 = jnp.where(ends_last, a_m * s_0 * a_0, s_0)
    C_1 = jnp.where(ends_last, a_0 * s_1 * a_1, s_1)
    s_own = jnp.where(first_core, s_0, s_1)
    a_before, s_before = jnp.where(first_core, a_m, a_0), jnp.where(first_core, s_m, s_0)
    a_after, s_after = jnp.where(first_core, a_1, a_p), jnp.where(first_core, s_1, s_p)
    k_1 = jnp.where(ends_last, s_own, a_after * s_own)
    k_2 = jnp.where(ends_last, own_a * s_before, s_after)
    k_3 = jnp.where(ends_last, a_before * s_own * s_own, s_own * s_own)
    k_4 = jnp.where(ends_last, a_before * s_own * k_2 + s_before * s_before, 0.0)
    flip_after = jnp.where(first_core, near[0, 8:16, :], near[1, 8:16, :]) == 1.0

    my_stat = stat.at[chip]
    my_stat[0] = A_0 * A_1
    my_stat[1] = R_0 * R_1
    my_stat[2] = C_0 + R_0 * C_1 * A_0
    for d in chip_order:
        send(my_stat, stat.at[chip], stat_sem.at[0], stat_sem.at[1], chip_peer(d))

    faces[0].wait()
    faces[1].wait()
    start_mask, end_mask = zero + not_start > 0.5, zero + not_end > 0.5

    def join_chain(n):
        for j in range(8):
            spot = n * 64 + 8 * j
            low, high = tile(s, n * 512 + 8 * j), tile(s, n * 512 + 448 + 8 * j)
            low[...] = jnp.where(start_mask, 0.5 * (low[...] + oriented(tile(got_l, spot)[...])), low[...])
            high[...] = jnp.where(end_mask, 0.5 * (high[...] + tile(got_r, spot)[...]), high[...])

    each(0, 3, join_chain)

    def divergence_plane(i):
        at_row = i * 64
        even, odd = split([strided(s, 1024 + at_row, k) for k in range(8)])
        for p in range(4):
            for k, slope in zip((p, 7 - p), apply_d(even, odd, p)):
                tt[8 * k : 8 * k + 8, :] = m[2] * slope
        even, odd = split([tile(s, 512 + at_row + 8 * j)[...] for j in range(8)])
        for p in range(4):
            for j, slope in zip((p, 7 - p), apply_d(even, odd, p)):
                tile(dv, at_row + 8 * j)[...] = m[1] * slope + strided(tt, 0, j)

    each(0, 8, divergence_plane)

    def guess_line(j):
        even, odd = split([tile(s, 64 * i + 8 * j)[...] for i in range(8)])
        nearer = jnp.minimum(j, 7 - j)
        for p in range(4):
            weight = tile(wgt, 8 * (4 * p + nearer))[...]
            for i, slope in zip((p, 7 - p), apply_d(even, odd, p)):
                spot = tile(dv, 64 * i + 8 * j)
                whole = spot[...] + m[0] * slope
                spot[...] = whole
                tile(fg, 64 * i + 8 * j)[...] = weight * whole

    each(0, 8, guess_line)

    def residual_plane(i):
        at_row = i * 64
        even, odd = split([strided(fg, at_row, k) for k in range(8)])
        for p in range(4):
            for k, bend in zip((p, 7 - p), apply_k(even, odd, p)):
                tt[8 * k : 8 * k + 8, :] = msq[2] * bend
        even, odd = split([tile(fg, at_row + 8 * j)[...] for j in range(8)])
        for p in range(4):
            for j, bend in zip((p, 7 - p), apply_k(even, odd, p)):
                at_j = at_row + 8 * j
                gone = tile(fg, at_j)[...] + msq[1] * bend + strided(tt, 0, j)
                tile(res, at_j)[...] = tile(dv, at_j)[...] - gone

    each(0, 8, residual_plane)

    def project_line(j):
        even, odd = split([tile(fg, 64 * i + 8 * j)[...] for i in range(8)])
        left = [None] * 8
        for p in range(4):
            for i, bend in zip((p, 7 - p), apply_k(even, odd, p)):
                left[i] = tile(res, 64 * i + 8 * j)[...] - msq[0] * bend
        low = high = None
        for i in range(1, 7):
            low = float(H[0, i]) * left[i] + (0.0 if low is None else low)
            high = float(H[1, i]) * left[i] + (0.0 if high is None else high)
        for n, part in enumerate((low, high, left[7], left[0])):
            tile(proj, n * 64 + 8 * j)[...] = part

    each(0, 8, project_line)

    gap = [by_row(H[0]), by_row(H[1])]
    sums = []
    for n in range(4):
        x = [proj[n * 64 + 8 * j : n * 64 + 8 * j + 8, :] for j in range(8)]
        shared = 0.5 * (x[0] + pltpu.roll(x[7], 1, 1))
        x[0], x[7] = shared, pltpu.roll(shared, 127, 1)
        modes = []
        for b in range(2):
            part = None
            for j in range(8):
                if H[b, j] != 0.0:
                    part = float(H[b, j]) * x[j] + (0.0 if part is None else part)
            for e in range(2):
                modes.append(jnp.sum(part * gap[e], axis=0, keepdims=True) * (1.0 / 64.0))
        sums.append(modes)

    def rows_of(values):
        out = zero
        for k, value in enumerate(values):
            out = jnp.where(row == k, value, out)
        return out

    inside = rows_of(sums[0] + sums[1])
    on_face = rows_of(sums[2] + sums[3])
    across_face = rows_of(sums[3] + sums[2])
    swapped = rows_of([part[e] for part in (sums[3], sums[2]) for e in (1, 0, 3, 2)])
    swap = jnp.where(ends_last, turned.astype(F32), flip_after.astype(F32)) > 0.5
    pushed = 0.5 * jnp.where(swap, swapped, across_face)
    own_share = jnp.where(ends_last, 1.0 - 0.5 * not_end, 1.0 - 0.5 * not_start)
    rhs = inside + own_share * on_face

    b_own = k_1 * rhs + k_2 * pushed
    d_own = k_3 * rhs + k_4 * pushed
    mine[0] = b_own
    mine[1] = d_own
    pair = send(mine, partner, pair_sem.at[0], pair_sem.at[1], other_core)
    pair.wait()
    B_0, D_0 = jnp.where(first_core, b_own, partner[0]), jnp.where(first_core, d_own, partner[1])
    B_1, D_1 = jnp.where(first_core, partner[0], b_own), jnp.where(first_core, partner[1], d_own)
    my_chip = chips.at[chip]
    my_chip[0] = A_1 * B_0 + B_1
    my_chip[1] = D_0 + R_0 * (C_1 * B_0 + D_1)
    for d in chip_order:
        send(my_chip, chips.at[chip], chip_sem.at[0], chip_sem.at[1], chip_peer(d))

    for i in range(8):
        join_span(fg, 64 * i)
    for j in range(8):
        tile(pface_l, 8 * j)[...] = oriented(tile(fg, 8 * j)[...])
        tile(pface_r, 8 * j)[...] = tile(fg, 448 + 8 * j)[...]
    pfaces = [
        send(pface_l, pgot_r, pface_send.at[0], pface_recv.at[0], before),
        send(pface_r, pgot_l, pface_send.at[1], pface_recv.at[1], after),
    ]
    faces[2].wait()
    faces[3].wait()
    each(3, 5, join_chain)
    adv_copy = pltpu.make_async_copy(s, adv_out, out_sem.at[0])
    adv_copy.start()

    wait_bytes(stat.at[0 : chips_n - 1], stat_sem.at[1])
    wait_bytes(stat.at[0 : chips_n - 1], stat_sem.at[0])

    def factors_up(n, up):
        pre[n, 0] = up
        return stat[n, 0] * up

    ones = zero + 1.0
    slab_a = lax.fori_loop(0, chips_n, factors_up, ones, unroll=4)

    def factors_down(t, carry):
        n = chips_n - 1 - t
        down, mixed = carry
        pre[n, 1] = down
        pre[n, 2] = mixed
        return stat[n, 1] * down, stat[n, 1] * mixed + stat[n, 2] * pre[n, 0]

    slab_r, slab_c = lax.fori_loop(0, chips_n, factors_down, (ones, zero), unroll=4)
    my_zstat = zstat.at[z]
    my_zstat[0] = slab_a
    my_zstat[1] = slab_r
    my_zstat[2] = slab_c
    for d in slab_order:
        send(my_zstat, zstat.at[z], zstat_sem.at[0], zstat_sem.at[1], slab_peer(d))

    for copy in pfaces:
        copy.wait()
    for j in range(8):
        low, high = tile(fg, 8 * j), tile(fg, 448 + 8 * j)
        low[...] = jnp.where(start_mask, 0.5 * (low[...] + oriented(tile(pgot_l, 8 * j)[...])), low[...])
        high[...] = jnp.where(end_mask, 0.5 * (high[...] + tile(pgot_r, 8 * j)[...]), high[...])

    wait_bytes(chips.at[0 : chips_n - 1], chip_sem.at[1])

    def chips_up(n, up):
        pre[n, 3] = up
        return stat[n, 0] * up + chips[n, 0]

    slab_b = lax.fori_loop(0, chips_n, chips_up, zero, unroll=4)

    def chips_down(t, down):
        n = chips_n - 1 - t
        pre[n, 4] = down
        return stat[n, 1] * down + (stat[n, 2] * pre[n, 3] + chips[n, 1])

    slab_d = lax.fori_loop(0, chips_n, chips_down, zero, unroll=4)
    my_slab = slabs.at[z]
    my_slab[0] = slab_b
    my_slab[1] = slab_d
    for d in slab_order:
        send(my_slab, slabs.at[z], slab_sem.at[0], slab_sem.at[1], slab_peer(d))

    wait_bytes(chips.at[0 : chips_n - 1], chip_sem.at[0])
    wait_bytes(zstat.at[0 : nz - 1], zstat_sem.at[0])
    wait_bytes(zstat.at[0 : nz - 1], zstat_sem.at[1])
    wait_bytes(slabs.at[0 : nz - 1], slab_sem.at[1])

    up, down = zero, zero
    for n in range(nz):
        kept[n, 0] = up
        up = zstat[n, 0] * up + slabs[n, 0]
    for n in range(nz - 1, -1, -1):
        kept[n, 1] = down
        down = zstat[n, 1] * down + (zstat[n, 2] * kept[n, 0] + slabs[n, 1])
    up, down = kept[z, 0], kept[z, 1]
    chip_up = pre[chip, 3] + pre[chip, 0] * up
    chip_down = pre[chip, 4] + pre[chip, 1] * down + pre[chip, 2] * up
    middle = A_0 * chip_up + B_0
    up = jnp.where(first_core, chip_up, middle)
    down = jnp.where(first_core, R_1 * chip_down + C_1 * middle + D_1, chip_down)
    back = jnp.where(
        ends_last, down + s_own * (own_a * up + b_own), own_a * down + s_own * (up + s_own * rhs)
    )

    modes = [jnp.broadcast_to(back[k : k + 1, :], (8, 128)) for k in range(8)]
    edges = [gap[0] * modes[2 * k] + gap[1] * modes[2 * k + 1] for k in range(4)]
    for j in range(8):
        ends = [float(H[0, j]) * edges[2 * a] + float(H[1, j]) * edges[2 * a + 1] for a in range(2)]
        for i in range(8):
            spot = tile(fg, 64 * i + 8 * j)
            spot[...] = spot[...] + float(H[0, i]) * ends[0] + float(H[1, i]) * ends[1]
    prs_copy = pltpu.make_async_copy(fg, prs_out, out_sem.at[1])
    prs_copy.start()
    wait_bytes(slabs.at[0 : nz - 1], slab_sem.at[0])
    adv_copy.wait()
    prs_copy.wait()


def solution(mesh):
    nz, sub_n = mesh.shape["slab"], mesh.shape["sub"]
    nx = 2 if sub_n == 8 else 4
    ny = sub_n // (2 * nx)
    vmem = lambda *shape: pltpu.VMEM(shape, F32)
    dma = lambda n: pltpu.SemaphoreType.DMA((n,))
    anywhere = pl.BlockSpec(memory_space=pl.ANY)

    def local(fields, metric, diffusivity, joule_heat, face_flip, coarse_decay):
        advanced, pressure = pl.pallas_call(
            functools.partial(kernel, (nz, nx, ny)),
            name="step",
            out_shape=(jax.ShapeDtypeStruct((2560, 128), F32), jax.ShapeDtypeStruct((512, 128), F32)),
            in_specs=[anywhere] * 6,
            out_specs=(anywhere, anywhere),
            scratch_shapes=[
                vmem(2560, 128),
                vmem(512, 128),
                vmem(3, 1, 128),
                pltpu.SMEM((5,), F32),
                pltpu.SMEM((1,), jnp.int32),
                vmem(8, 128),
                vmem(2560, 128),
                vmem(1536, 128),
                vmem(64, 128),
                vmem(512, 128),
                vmem(512, 128),
                vmem(512, 128),
                vmem(128, 128),
                vmem(256, 128),
                vmem(nz, 2, 8, 128),
                vmem(320, 128),
                vmem(320, 128),
                vmem(320, 128),
                vmem(320, 128),
                vmem(64, 128),
                vmem(64, 128),
                vmem(64, 128),
                vmem(64, 128),
                vmem(16, 128),
                vmem(3, 16, 128),
                vmem(2, 8, 128),
                vmem(2, 8, 128),
                vmem(nx * ny, 2, 8, 128),
                vmem(nx * ny, 3, 8, 128),
                vmem(nx * ny, 5, 8, 128),
                vmem(nz, 2, 8, 128),
                vmem(nz, 3, 8, 128),
                dma(6), dma(2), dma(4), dma(4), dma(2), dma(2), dma(3), dma(3),
                dma(2), dma(2), dma(2), dma(2), dma(2),
            ],
            compiler_params=pltpu.CompilerParams(
                collective_id=0, has_side_effects=True, vmem_limit_bytes=32 * 1024 * 1024
            ),
        )(
            fields.reshape(2560, 128), joule_heat.reshape(512, 128), metric, diffusivity,
            face_flip, coarse_decay.reshape(8, 128),
        )
        return advanced.reshape(5, 512, 1, 128), pressure.reshape(512, 1, 128)

    in_specs = (
        P(None, None, ("slab", "sub"), None),
        P(None, ("slab", "sub"), None),
        P(),
        P(None, ("slab", "sub"), None),
        P(("slab", "sub")),
        P(None, ("slab", "sub"), None),
    )
    out_specs = (P(None, None, ("slab", "sub"), None), P(None, ("slab", "sub"), None))
    return jax.shard_map(local, mesh=mesh, in_specs=in_specs, out_specs=out_specs, check_vma=False)
```

```python
import functools

import jax
import jax.numpy as jnp
import numpy as np
from jax import lax
from jax.experimental import pallas as pl
from jax.experimental.pallas import tpu as pltpu
from jax.sharding import PartitionSpec as P

MESH = pl.DeviceIdType.MESH
F32 = jnp.float32

POINTS = np.cos(np.pi * np.arange(8) / 7.0)


def derivative():
    endings = np.ones(8)
    endings[0] = endings[7] = 2.0
    weighted = endings * (-1.0) ** np.arange(8)
    spacing = POINTS[:, None] - POINTS[None, :] + np.eye(8)
    derive = weighted[:, None] / weighted[None, :] / spacing
    return derive - np.eye(8) * np.sum(derive, axis=1)[:, None]


D = derivative()
K = D.T @ D
COLUMN_SQ = np.sum(D * D, axis=0)
H = np.stack([(1.0 - POINTS) / 2.0, (1.0 + POINTS) / 2.0])


def half_tables(matrix):
    even = (matrix[:4, :4] + matrix[:4, :3:-1]) / 2.0
    odd = (matrix[:4, :4] - matrix[:4, :3:-1]) / 2.0
    return even.tolist(), odd.tolist()


D_EVEN, D_ODD = half_tables(D)
K_EVEN, K_ODD = half_tables(K)


def dot4(row, parts):
    total = row[0] * parts[0]
    for a in range(1, 4):
        total = total + row[a] * parts[a]
    return total


def split(x):
    return [x[a] + x[7 - a] for a in range(4)], [x[a] - x[7 - a] for a in range(4)]


def apply_d(even, odd, p):
    from_even, from_odd = dot4(D_EVEN[p], even), dot4(D_ODD[p], odd)
    return from_odd + from_even, from_odd - from_even


def apply_k(even, odd, p):
    from_even, from_odd = dot4(K_EVEN[p], even), dot4(K_ODD[p], odd)
    return from_even + from_odd, from_even - from_odd


def ring(n, d):
    return min(d, n - d)


def kernel(
    sizes, fields, heat, metric, diffusivity, flip, decay, adv_out, guess_out, back_out,
    f, q, met, dif, flp, dec, s, u, tt, dv, fg, res, wgt, proj,
    face_l, face_r, got_l, got_r, pface_l, pface_r, pgot_l, pgot_r,
    near_out, near, mine, partner, rates, edge, backs,
    y_stat, y_push, y_pre, x_stat, x_push, x_pre, z_stat, z_push, z_pre,
    load_sem, out_sem, face_send, face_recv, pface_send, pface_recv, near_send, near_recv,
    pair_sem, rate_sem, swap_sem, edge_send, edge_recv, push_send, push_recv, stat_send, stat_recv,
    stat_tail_send, stat_tail_recv, push_tail_send, push_tail_recv, heard,
):
    nz, nx, ny = sizes
    chips_n = nx * ny
    sub_n = 2 * chips_n
    total = nz * sub_n
    z, sub = lax.axis_index("slab"), lax.axis_index("sub")
    core = lax.rem(sub, 2)
    chip = lax.div(sub, 2)
    cx, cy = lax.div(chip, ny), lax.rem(chip, ny)
    here = z * sub_n + sub
    at_start, at_end = here == 0, here == total - 1
    side = 2 * core - 1

    def at(position):
        position = lax.rem(position + total, total)
        return (lax.div(position, sub_n), lax.rem(position, sub_n))

    other_core = (z, sub - side)
    before, after = at(here - 1), at(here + 1)
    outer, outer_two, inner_two = at(here + side), at(here + 2 * side), at(here - 2 * side)
    chip_at = z * chips_n + chip
    more_before, more_after = chip_at > 0, chip_at < nz * chips_n - 1
    has_outer = jnp.where(core == 0, more_before, more_after)
    has_inner = jnp.where(core == 0, more_after, more_before)
    by_distance = lambda n: sorted(range(1, n), key=lambda d: -ring(n, d))
    y_order, x_order, z_order = by_distance(ny), by_distance(nx), by_distance(nz)

    def shift(dx, dy, dz):
        px, py = lax.rem(cx + dx + nx, nx), lax.rem(cy + dy + ny, ny)
        return (lax.rem(z + dz + nz, nz), (px * ny + py) * 2 + core)

    y_peers = [shift(0, d, 0) for d in y_order]
    x_peers = [shift(d, 0, 0) for d in x_order]
    z_peers = [shift(0, 0, d) for d in z_order]

    def remote(src, dst, send_sem, recv_sem, device):
        return pltpu.make_async_remote_copy(
            src_ref=src, dst_ref=dst, send_sem=send_sem, recv_sem=recv_sem,
            device_id=device, device_id_type=MESH,
        )

    def send(*args):
        copy = remote(*args)
        copy.start()
        return copy

    def when(condition, action):
        if condition is None:
            action()
        else:
            pl.when(condition)(action)

    class Exchange:
        def __init__(self, parts):
            self.parts = [(sent, got, remote(*args)) for sent, got, args in parts]

        def start(self):
            for sent, _, copy in self.parts:
                when(sent, copy.start)

        def wait(self):
            for sent, got, copy in self.parts:
                when(got, copy.wait_recv)
                when(sent, copy.wait_send)

    def wait_bytes(ref, sem):
        pltpu.make_async_copy(ref, ref, sem).wait()

    loads = [
        pltpu.make_async_copy(decay, dec, load_sem.at[0]),
        pltpu.make_async_copy(metric, met, load_sem.at[1]),
        pltpu.make_async_copy(flip, flp, load_sem.at[2]),
        pltpu.make_async_copy(diffusivity, dif, load_sem.at[3]),
        pltpu.make_async_copy(heat, q, load_sem.at[4]),
    ]
    for n in range(5):
        spot = pl.ds(512 * n, 512)
        loads.append(pltpu.make_async_copy(fields.at[spot], f.at[spot], load_sem.at[5 + n]))
    for copy in loads:
        copy.start()

    def offsets(n, wanted):
        return sorted({d % n for d in wanted} - {0})

    near_x = offsets(nx, (1, 2, 3))
    near_y = offsets(ny, (1, 2, -1, -2))
    near_z = offsets(nz, (1, 2, -1, -2))
    barrier = pltpu.get_barrier_semaphore()
    targets = [other_core] + [shift(d, 0, 0) for d in near_x]
    targets += [shift(0, d, 0) for d in near_y] + [shift(0, 0, d) for d in near_z]
    for device in targets:
        pl.semaphore_signal(barrier, inc=1, device_id=device, device_id_type=MESH)
    for condition, device in ((has_outer, outer), (has_inner, inner_two)):

        @pl.when(condition)
        def _():
            pl.semaphore_signal(barrier, inc=1, device_id=device, device_id_type=MESH)

    second = [shift(0, d, 0) for d in offsets(ny, (2, -2))] + [shift(0, 0, d) for d in offsets(nz, (2, -2))]
    third = [shift(0, 0, d) for d in offsets(nz, (4, -4))]

    def pass_word(k, devices):
        for device in devices:
            pl.semaphore_signal(heard.at[k], inc=1, device_id=device, device_id_type=MESH)

    for copy in loads:
        copy.wait()

    row = lax.broadcasted_iota(jnp.int32, (8, 128), 0)
    zero = jnp.zeros((8, 128), F32)
    wall = jnp.where((row == 0) | (row == 7), 0.0, 1.0)
    turned = (zero + flp[0].astype(F32)) == 1.0
    m = [jnp.broadcast_to(met[d], (8, 128)) for d in range(3)]
    msq = [m[d] * m[d] for d in range(3)]

    def by_row(values):
        out = zero + float(values[7])
        for k in range(7):
            out = jnp.where(row == k, float(values[k]), out)
        return out

    def reverse(x):
        half = pltpu.roll(x, 4, 0)
        pairs = jnp.where(lax.rem(row, 4) < 2, pltpu.roll(half, 6, 0), pltpu.roll(half, 2, 0))
        return jnp.where(lax.rem(row, 2) == 0, pltpu.roll(pairs, 7, 0), pltpu.roll(pairs, 1, 0))

    def oriented(x):
        return jnp.where(turned, reverse(x), x)

    def tile(ref, base):
        return ref.at[pl.ds(pl.multiple_of(base, 8), 8), :]

    def strided(ref, base, k):
        return ref[pl.ds(base + k, 8, stride=8), :]

    def start_plane(i):
        def line(j, carry):
            at_row = i * 64 + j * 8
            x = [tile(f, n * 512 + at_row)[...] for n in range(5)]
            warm = jnp.tanh(x[3])
            bubbles = jnp.tanh(0.5 * x[4])
            heating = tile(q, at_row)[...] * (0.05 + 0.025 * warm) * (0.5 - 0.5 * bubbles)
            lifting = 0.015 * x[3] - 0.0125 - 0.0125 * bubbles
            added = [x[0], x[1] + lifting, x[2], x[3] + heating, x[4] + 0.2 * heating]
            for n in range(5):
                tile(s, n * 512 + at_row)[...] = added[n]
            for n in range(3):
                tile(u, n * 512 + at_row)[...] = 0.01 * m[n] * x[n]
            return carry

        lax.fori_loop(0, 8, line, 0, unroll=2)

    def step_plane(n, i):
        at_row = i * 64
        base = n * 512 + at_row
        rate = dif[n]
        c1, c2 = rate * msq[1], rate * msq[2]
        even, odd = split([strided(f, base, k) for k in range(8)])
        for p in range(4):
            slopes, bends = apply_d(even, odd, p), apply_k(even, odd, p)
            for k, slope, bend in zip((p, 7 - p), slopes, bends):
                tt[8 * k : 8 * k + 8, :] = strided(u, 1024 + at_row, k) * slope + c2 * bend
        even, odd = split([tile(f, base + 8 * j)[...] for j in range(8)])
        for p in range(4):
            slopes, bends = apply_d(even, odd, p), apply_k(even, odd, p)
            for j, slope, bend in zip((p, 7 - p), slopes, bends):
                gone = tile(u, 512 + at_row + 8 * j)[...] * slope + c1 * bend
                gone = gone + strided(tt, 0, j)
                tile(s, base + 8 * j)[...] = tile(s, base + 8 * j)[...] - gone

    def step_lines(n, pairs):
        c0 = dif[n] * msq[0]
        keep = jnp.where(zero + (n < 3).astype(F32) > 0.5, wall, 1.0)

        def line(j, carry):
            base = n * 512 + j * 8
            even, odd = split([tile(f, base + 64 * i)[...] for i in range(8)])
            for p in pairs:
                slopes, bends = apply_d(even, odd, p), apply_k(even, odd, p)
                for i, slope, bend in zip((p, 7 - p), slopes, bends):
                    gone = tile(u, i * 64 + j * 8)[...] * slope + c0 * bend
                    tile(s, base + 64 * i)[...] = keep * (tile(s, base + 64 * i)[...] - gone)
            return carry

        lax.fori_loop(0, 8, line, 0, unroll=2)

    def join_span(ref, base):
        low, high = tile(ref, base), tile(ref, base + 56)
        shared = 0.5 * (low[...] + pltpu.roll(high[...], 1, 1))
        low[...] = shared
        high[...] = pltpu.roll(shared, 127, 1)

    def stage_faces(n):
        for j in range(8):
            spot = n * 64 + 8 * j
            tile(face_l, spot)[...] = oriented(tile(s, n * 512 + 8 * j)[...])
            tile(face_r, spot)[...] = tile(s, n * 512 + 448 + 8 * j)[...]

    def each(low, high, body):
        def run(n, carry):
            body(n)
            return carry

        lax.fori_loop(low, high, run, 0)

    near_out[0:8, :] = dec[...]
    near_out[8:16, :] = zero + flp[0].astype(F32)

    for i in (0, 7):
        start_plane(i)

    def velocity_faces(n):
        for i in (0, 7):
            step_plane(n, i)
        step_lines(n, (0,))
        for i in (0, 7):
            join_span(s, n * 512 + i * 64)
        stage_faces(n)

    each(0, 2, velocity_faces)

    pl.semaphore_wait(barrier, len(targets) + 2 * has_outer.astype(jnp.int32))
    pass_word(0, second)
    nears = Exchange([
        (None, None, (near_out, near.at[0], near_send.at[0], near_recv.at[0], other_core)),
        (has_outer, has_outer, (near_out, near.at[1], near_send.at[1], near_recv.at[1], outer)),
        (has_outer, has_inner, (near_out, near.at[2], near_send.at[2], near_recv.at[2], outer_two)),
    ])
    nears.start()
    for condition, k in ((has_outer, 1), (has_inner, 2)):

        @pl.when(jnp.logical_not(condition))
        def _():
            near[k] = jnp.zeros((16, 128), F32)

    each(2, 3, velocity_faces)

    def chain_exchange(left, right, from_left, from_right, sems, k):
        ahead, behind = jnp.logical_not(at_end), jnp.logical_not(at_start)
        return Exchange([
            (behind, ahead, (left, from_right, sems[0].at[k], sems[1].at[k], before)),
            (ahead, behind, (right, from_left, sems[0].at[k + 1], sems[1].at[k + 1], after)),
        ])

    part = slice(0, 192)
    velocity_exchange = chain_exchange(
        face_l.at[part], face_r.at[part], got_l.at[part], got_r.at[part], (face_send, face_recv), 0
    )
    velocity_exchange.start()

    for p in (1, 2, 3):
        for i in (p, 7 - p):
            start_plane(i)

    def velocity_rest(n):
        def plane(i, carry):
            step_plane(n, i)
            return carry

        lax.fori_loop(1, 7, plane, 0)
        step_lines(n, (1, 2, 3))
        for i in range(1, 7):
            join_span(s, n * 512 + i * 64)

    each(0, 2, velocity_rest)
    pl.semaphore_wait(heard.at[0], len(second))
    pass_word(1, third)
    rates[core, cy + 1] = dec[...]
    for device in y_peers:
        send(dec, rates.at[core, cy + 1], rate_sem.at[0], rate_sem.at[1], device)
    each(2, 3, velocity_rest)

    across = msq[2] * by_row(COLUMN_SQ) + 1.0
    for a in range(4):
        for b in range(4):
            under = across + (float(COLUMN_SQ[a]) * msq[0] + float(COLUMN_SQ[b]) * msq[1])
            wgt[8 * (4 * a + b) : 8 * (4 * a + b) + 8, :] = 0.5 / under

    nears.wait()
    own_a, partner_a, outer_a, far_a = dec[...], near[0, 0:8, :], near[1, 0:8, :], near[2, 0:8, :]
    first_core = zero + core.astype(F32) < 0.5
    not_start = 1.0 - at_start.astype(F32)
    not_end = 1.0 - at_end.astype(F32)
    a_0, a_1 = jnp.where(first_core, own_a, partner_a), jnp.where(first_core, partner_a, own_a)
    a_m, a_p = jnp.where(first_core, outer_a, far_a), jnp.where(first_core, far_a, outer_a)
    chip_first = (z * chips_n + chip == 0).astype(F32)
    chip_last = (z * chips_n + chip == nz * chips_n - 1).astype(F32)

    def root(a):
        return jnp.sqrt((1.0 - a) * (1.0 + a))

    s_0, s_1 = root(a_0), root(a_1)
    s_m, s_p = (1.0 - chip_first) * root(a_m), (1.0 - chip_last) * root(a_p)
    a_m, a_p = (1.0 - chip_first) * a_m, (1.0 - chip_last) * a_p

    edge[0] = a_m
    edge[1] = a_p
    ends = ((cy == 0, 0, (1, 0)), (cy == ny - 1, 1, (0, ny + 1)))
    for is_end, k, place in ends:

        @pl.when(is_end)
        def _():
            rates[place] = edge[k]
            for device in y_peers:
                send(edge.at[k], rates.at[place], edge_send.at[k], edge_recv.at[k], device)

    ends_last = row < 4
    A_0, A_1 = jnp.where(ends_last, a_0, a_1), jnp.where(ends_last, a_1, a_p)
    R_0, R_1 = jnp.where(ends_last, a_m, a_0), jnp.where(ends_last, a_0, a_1)
    C_1 = jnp.where(ends_last, a_0 * s_1 * a_1, s_1)
    s_own = jnp.where(first_core, s_0, s_1)
    a_before, s_before = jnp.where(first_core, a_m, a_0), jnp.where(first_core, s_m, s_0)
    a_after, s_after = jnp.where(first_core, a_1, a_p), jnp.where(first_core, s_1, s_p)
    k_1 = jnp.where(ends_last, s_own, a_after * s_own)
    k_2 = jnp.where(ends_last, own_a * s_before, s_after)
    k_3 = jnp.where(ends_last, a_before * s_own * s_own, s_own * s_own)
    k_4 = jnp.where(ends_last, a_before * s_own * k_2 + s_before * s_before, 0.0)
    flip_after = jnp.where(first_core, near[0, 8:16, :], near[1, 8:16, :]) == 1.0

    velocity_exchange.wait()
    start_mask, end_mask = zero + not_start > 0.5, zero + not_end > 0.5

    def join_chain(n):
        for j in range(8):
            spot = n * 64 + 8 * j
            low, high = tile(s, n * 512 + 8 * j), tile(s, n * 512 + 448 + 8 * j)
            low[...] = jnp.where(start_mask, 0.5 * (low[...] + oriented(tile(got_l, spot)[...])), low[...])
            high[...] = jnp.where(end_mask, 0.5 * (high[...] + tile(got_r, spot)[...]), high[...])

    each(0, 3, join_chain)

    def divergence_plane(i):
        at_row = i * 64
        even, odd = split([strided(s, 1024 + at_row, k) for k in range(8)])
        for p in range(4):
            for k, slope in zip((p, 7 - p), apply_d(even, odd, p)):
                tt[8 * k : 8 * k + 8, :] = m[2] * slope
        even, odd = split([tile(s, 512 + at_row + 8 * j)[...] for j in range(8)])
        for p in range(4):
            for j, slope in zip((p, 7 - p), apply_d(even, odd, p)):
                tile(dv, at_row + 8 * j)[...] = m[1] * slope + strided(tt, 0, j)

    each(0, 8, divergence_plane)

    def guess_line(j):
        even, odd = split([tile(s, 64 * i + 8 * j)[...] for i in range(8)])
        nearer = jnp.minimum(j, 7 - j)
        for p in range(4):
            weight = tile(wgt, 8 * (4 * p + nearer))[...]
            for i, slope in zip((p, 7 - p), apply_d(even, odd, p)):
                spot = tile(dv, 64 * i + 8 * j)
                whole = spot[...] + m[0] * slope
                spot[...] = whole
                tile(fg, 64 * i + 8 * j)[...] = weight * whole

    each(0, 8, guess_line)

    def residual_plane(i):
        at_row = i * 64
        even, odd = split([strided(fg, at_row, k) for k in range(8)])
        for p in range(4):
            for k, bend in zip((p, 7 - p), apply_k(even, odd, p)):
                tt[8 * k : 8 * k + 8, :] = msq[2] * bend
        even, odd = split([tile(fg, at_row + 8 * j)[...] for j in range(8)])
        for p in range(4):
            for j, bend in zip((p, 7 - p), apply_k(even, odd, p)):
                at_j = at_row + 8 * j
                gone = tile(fg, at_j)[...] + msq[1] * bend + strided(tt, 0, j)
                tile(res, at_j)[...] = tile(dv, at_j)[...] - gone

    each(0, 8, residual_plane)

    def project_line(j):
        even, odd = split([tile(fg, 64 * i + 8 * j)[...] for i in range(8)])
        left = [None] * 8
        for p in range(4):
            for i, bend in zip((p, 7 - p), apply_k(even, odd, p)):
                left[i] = tile(res, 64 * i + 8 * j)[...] - msq[0] * bend
        low = high = None
        for i in range(1, 7):
            low = float(H[0, i]) * left[i] + (0.0 if low is None else low)
            high = float(H[1, i]) * left[i] + (0.0 if high is None else high)
        for n, part in enumerate((low, high, left[7], left[0])):
            tile(proj, n * 64 + 8 * j)[...] = part

    each(0, 8, project_line)

    gap = [by_row(H[0]), by_row(H[1])]
    sums = []
    for n in range(4):
        x = [proj[n * 64 + 8 * j : n * 64 + 8 * j + 8, :] for j in range(8)]
        shared = 0.5 * (x[0] + pltpu.roll(x[7], 1, 1))
        x[0], x[7] = shared, pltpu.roll(shared, 127, 1)
        modes = []
        for b in range(2):
            part = None
            for j in range(8):
                if H[b, j] != 0.0:
                    part = float(H[b, j]) * x[j] + (0.0 if part is None else part)
            for e in range(2):
                modes.append(jnp.sum(part * gap[e], axis=0, keepdims=True) * (1.0 / 64.0))
        sums.append(modes)

    def rows_of(values):
        out = zero
        for k, value in enumerate(values):
            out = jnp.where(row == k, value, out)
        return out

    inside = rows_of(sums[0] + sums[1])
    on_face = rows_of(sums[2] + sums[3])
    across_face = rows_of(sums[3] + sums[2])
    swapped = rows_of([part[e] for part in (sums[3], sums[2]) for e in (1, 0, 3, 2)])
    swap = jnp.where(ends_last, turned.astype(F32), flip_after.astype(F32)) > 0.5
    pushed = 0.5 * jnp.where(swap, swapped, across_face)
    own_share = jnp.where(ends_last, 1.0 - 0.5 * not_end, 1.0 - 0.5 * not_start)
    rhs = inside + own_share * on_face

    b_own = k_1 * rhs + k_2 * pushed
    d_own = k_3 * rhs + k_4 * pushed
    mine[0] = b_own
    mine[1] = d_own
    pair = send(mine, partner, pair_sem.at[0], pair_sem.at[1], other_core)
    pair.wait()
    B_0, D_0 = jnp.where(first_core, b_own, partner[0]), jnp.where(first_core, d_own, partner[1])
    B_1, D_1 = jnp.where(first_core, partner[0], b_own), jnp.where(first_core, partner[1], d_own)
    y_push[cy, 0] = A_1 * B_0 + B_1
    y_push[cy, 1] = D_0 + R_0 * (C_1 * B_0 + D_1)

    def spread(ref, place, k, sems, devices):
        for device in devices:
            send(ref.at[place], ref.at[place], sems[0].at[k], sems[1].at[k], device)

    def spread_ended(ref, k, sem, devices):
        wait_bytes(ref.at[0 : len(devices)], sem.at[k])

    pushes, stats = (push_send, push_recv), (stat_send, stat_recv)
    def spread_z(ref, first, sems, k, tail_sems):
        rest = pl.ds(first, ref.shape[1] - first)
        for d, device in zip(z_order, z_peers):
            head = ref.at[z, pl.ds(0, first)]
            send(head, head, sems[0].at[k], sems[1].at[k], device)

            @pl.when(z + d >= nz)
            def _():
                tail = ref.at[z, rest]
                send(tail, tail, tail_sems[0].at[d], tail_sems[1].at[z], device)

    def spread_z_got(ref, first, sem, k, tail_sem):
        rest = pl.ds(first, ref.shape[1] - first)
        wait_bytes(ref.at[0 : nz - 1, pl.ds(0, first)], sem.at[k])
        for n in range(1, nz):

            @pl.when(z < n)
            def _():
                wait_bytes(ref.at[n, rest], tail_sem.at[n])

    def spread_z_left(ref, first, sem, k, tail_sem):
        rest = pl.ds(first, ref.shape[1] - first)
        wait_bytes(ref.at[0 : nz - 1, pl.ds(0, first)], sem.at[k])
        for d in range(1, nz):

            @pl.when(z + d >= nz)
            def _():
                wait_bytes(ref.at[z, rest], tail_sem.at[d])

    z_stat_tail, z_push_tail = (stat_tail_send, stat_tail_recv), (push_tail_send, push_tail_recv)
    spread(y_push, cy, 0, pushes, y_peers)

    wait_bytes(rates.at[core, pl.ds(1, ny - 1)], rate_sem.at[1])
    half = rates.at[core, pl.ds(1, ny)]
    swap_halves = send(half, half, swap_sem.at[0], swap_sem.at[1], other_core)
    for is_end, k, place in ends:

        @pl.when(jnp.logical_not(is_end))
        def _():
            wait_bytes(rates.at[place], edge_recv.at[k])

    swap_halves.wait()

    roots = [[root(rates[c, n + 1]) for n in range(ny)] for c in range(2)]
    for n in range(ny):
        e_m, e_0 = rates[1, n], rates[0, n + 1]
        e_1, e_p = rates[1, n + 1], rates[0, n + 2]
        both, lead = e_0 * e_1, e_m * e_0
        mixed = roots[0][n] + both * roots[1][n]
        y_stat[n, 0] = jnp.where(ends_last, both, e_1 * e_p)
        y_stat[n, 1] = jnp.where(ends_last, lead, both)
        y_stat[n, 2] = jnp.where(ends_last, lead * mixed, mixed)

    ones = zero + 1.0

    def combine_stat(stat, pre, count):
        up = ones
        for n in range(count):
            pre[n, 0] = up
            up = stat[n, 0] * up
        down, mixed = ones, zero
        for n in range(count - 1, -1, -1):
            pre[n, 1] = down
            pre[n, 2] = mixed
            mixed = stat[n, 1] * mixed + stat[n, 2] * pre[n, 0]
            down = stat[n, 1] * down
        return up, down, mixed

    def combine_push(stat, push, pre, count):
        up = zero
        for n in range(count):
            pre[n, 3] = up
            up = stat[n, 0] * up + push[n, 0]
        down = zero
        for n in range(count - 1, -1, -1):
            pre[n, 4] = down
            down = stat[n, 1] * down + (stat[n, 2] * pre[n, 3] + push[n, 1])
        return up, down

    def set_stat(ref, place, values):
        for k, value in enumerate(values):
            ref[place, k] = value

    set_stat(x_stat, cx, combine_stat(y_stat, y_pre, ny))
    spread(x_stat, cx, 0, stats, x_peers)

    def scalars(n):
        def plane(i, carry):
            step_plane(n, i)
            return carry

        lax.fori_loop(0, 8, plane, 0)
        step_lines(n, (0, 1, 2, 3))
        for i in range(8):
            join_span(s, n * 512 + i * 64)
        stage_faces(n)

    each(3, 5, scalars)
    for i in range(8):
        join_span(fg, 64 * i)
    for j in range(8):
        tile(pface_l, 8 * j)[...] = oriented(tile(fg, 8 * j)[...])
        tile(pface_r, 8 * j)[...] = tile(fg, 448 + 8 * j)[...]

    pl.semaphore_wait(heard.at[1], len(third)) if third else None
    spread_ended(x_stat, 0, stat_recv, x_peers)
    set_stat(z_stat, z, combine_stat(x_stat, x_pre, nx))
    spread_z(z_stat, 1, stats, 1, z_stat_tail)

    spread_ended(y_push, 0, push_recv, y_peers)
    set_stat(x_push, cx, combine_push(y_stat, y_push, y_pre, ny))
    spread(x_push, cx, 1, pushes, x_peers)
    guess_exchange = chain_exchange(pface_l, pface_r, pgot_l, pgot_r, (pface_send, pface_recv), 0)
    guess_exchange.start()
    part = slice(192, 320)
    scalar_exchange = chain_exchange(
        face_l.at[part], face_r.at[part], got_l.at[part], got_r.at[part], (face_send, face_recv), 2
    )
    scalar_exchange.start()
    spread_ended(x_push, 1, push_recv, x_peers)
    set_stat(z_push, z, combine_push(x_stat, x_push, x_pre, nx))
    spread_z(z_push, 1, pushes, 2, z_push_tail)
    wait_bytes(rates.at[core, pl.ds(1, ny - 1)], rate_sem.at[0])
    spread_ended(y_push, 0, push_send, y_peers)
    spread_ended(x_stat, 0, stat_send, x_peers)
    spread_ended(x_push, 1, push_send, x_peers)
    for is_end, k, place in ends:

        @pl.when(is_end)
        def _():
            wait_bytes(rates.at[0, pl.ds(1, ny - 1)], edge_send.at[k])

    guess_exchange.wait()
    for j in range(8):
        low, high = tile(fg, 8 * j), tile(fg, 448 + 8 * j)
        low[...] = jnp.where(start_mask, 0.5 * (low[...] + oriented(tile(pgot_l, 8 * j)[...])), low[...])
        high[...] = jnp.where(end_mask, 0.5 * (high[...] + tile(pgot_r, 8 * j)[...]), high[...])
    scalar_exchange.wait()
    each(3, 5, join_chain)
    adv_copy = pltpu.make_async_copy(s, adv_out, out_sem.at[0])
    adv_copy.start()

    guess_copy = pltpu.make_async_copy(fg, guess_out, out_sem.at[1])
    guess_copy.start()

    spread_z_got(z_stat, 1, stat_recv, 1, stat_tail_recv)
    spread_z_got(z_push, 1, push_recv, 2, push_tail_recv)

    up = zero
    for n in range(nz):
        z_pre[n, 3] = up
        up = z_stat[n, 0] * up + z_push[n, 0]
    down = zero
    for n in range(nz - 1, -1, -1):
        further = z_stat[n, 1] * down + (z_stat[n, 2] * z_pre[n, 3] + z_push[n, 1])
        down = jnp.where(zero + (n > z).astype(F32) > 0.5, further, zero)
        z_pre[n, 4] = down
    up = z_pre[z, 3]
    down = z_pre[lax.rem(z + 1, nz), 4]
    down = jnp.where(zero + (z + 1 < nz).astype(F32) > 0.5, down, zero)
    for pre, place in ((x_pre, cx), (y_pre, cy)):
        down = pre[place, 4] + pre[place, 1] * down + pre[place, 2] * up
        up = pre[place, 3] + pre[place, 0] * up
    chip_up, chip_down = up, down
    middle = A_0 * chip_up + B_0
    up = jnp.where(first_core, chip_up, middle)
    down = jnp.where(first_core, R_1 * chip_down + C_1 * middle + D_1, chip_down)
    back = jnp.where(
        ends_last, down + s_own * (own_a * up + b_own), own_a * down + s_own * (up + s_own * rhs)
    )

    backs[...] = back
    back_copy = pltpu.make_async_copy(backs, back_out, out_sem.at[2])
    back_copy.start()
    spread_z_left(z_stat, 1, stat_send, 1, stat_tail_send)
    spread_z_left(z_push, 1, push_send, 2, push_tail_send)
    adv_copy.wait()
    guess_copy.wait()
    back_copy.wait()


def finish(adv, guess, back, adv_out, prs_out, whole, fg, bk, sem):
    loads = [
        pltpu.make_async_copy(back, bk, sem.at[0]),
        pltpu.make_async_copy(guess, fg, sem.at[1]),
    ]
    come, go = [], []
    for n in range(5):
        spot = pl.ds(512 * n, 512)
        come.append(pltpu.make_async_copy(adv.at[spot], whole.at[spot], sem.at[3 + n]))
        go.append(pltpu.make_async_copy(whole.at[spot], adv_out.at[spot], sem.at[8 + n]))
    for copy in loads + come:
        copy.start()
    row = lax.broadcasted_iota(jnp.int32, (8, 128), 0)
    gap = []
    for b in range(2):
        values = jnp.full((8, 128), float(H[b, 7]), F32)
        for k in range(7):
            values = jnp.where(row == k, float(H[b, k]), values)
        gap.append(values)
    for copy in loads:
        copy.wait()
    modes = [jnp.broadcast_to(bk[k : k + 1, :], (8, 128)) for k in range(8)]
    edges = [gap[0] * modes[2 * k] + gap[1] * modes[2 * k + 1] for k in range(4)]
    for j in range(8):
        rims = [float(H[0, j]) * edges[2 * a] + float(H[1, j]) * edges[2 * a + 1] for a in range(2)]
        for i in range(8):
            at_ij = 64 * i + 8 * j
            guessed = fg[at_ij : at_ij + 8, :]
            fg[at_ij : at_ij + 8, :] = guessed + float(H[0, i]) * rims[0] + float(H[1, i]) * rims[1]
    out = pltpu.make_async_copy(fg, prs_out, sem.at[2])
    out.start()
    for n in range(5):
        come[n].wait()
        go[n].start()
    for copy in go:
        copy.wait()
    out.wait()


def solution(mesh):
    nz, sub_n = mesh.shape["slab"], mesh.shape["sub"]
    nx = 2 if sub_n == 8 else 4
    ny = sub_n // (2 * nx)
    vmem = lambda *shape: pltpu.VMEM(shape, F32)
    dma = lambda n: pltpu.SemaphoreType.DMA((n,))
    anywhere = pl.BlockSpec(memory_space=pl.ANY)

    def local(fields, metric, diffusivity, joule_heat, face_flip, coarse_decay):
        fields_shape = jax.ShapeDtypeStruct((2560, 128), F32)
        node_shape = jax.ShapeDtypeStruct((512, 128), F32)
        mode_shape = jax.ShapeDtypeStruct((8, 128), F32)
        advanced, guess, back = pl.pallas_call(
            functools.partial(kernel, (nz, nx, ny)),
            name="step",
            out_shape=(fields_shape, node_shape, mode_shape),
            in_specs=[anywhere] * 6,
            out_specs=(anywhere, anywhere, anywhere),
            scratch_shapes=[
                vmem(2560, 128),
                vmem(512, 128),
                vmem(3, 1, 128),
                pltpu.SMEM((5,), F32),
                pltpu.SMEM((1,), jnp.int32),
                vmem(8, 128),
                vmem(2560, 128),
                vmem(1536, 128),
                vmem(64, 128),
                vmem(512, 128),
                vmem(512, 128),
                vmem(512, 128),
                vmem(128, 128),
                vmem(256, 128),
                vmem(320, 128),
                vmem(320, 128),
                vmem(320, 128),
                vmem(320, 128),
                vmem(64, 128),
                vmem(64, 128),
                vmem(64, 128),
                vmem(64, 128),
                vmem(16, 128),
                vmem(3, 16, 128),
                vmem(2, 8, 128),
                vmem(2, 8, 128),
                vmem(2, ny + 2, 8, 128),
                vmem(2, 8, 128),
                vmem(8, 128),
                vmem(ny, 3, 8, 128), vmem(ny, 2, 8, 128), vmem(ny, 5, 8, 128),
                vmem(nx, 3, 8, 128), vmem(nx, 2, 8, 128), vmem(nx, 5, 8, 128),
                vmem(nz, 3, 8, 128), vmem(nz, 2, 8, 128), vmem(nz, 5, 8, 128),
                dma(10), dma(3), dma(4), dma(4), dma(2), dma(2), dma(3), dma(3),
                dma(2), dma(2), dma(2), dma(2), dma(2), dma(3), dma(3), dma(2), dma(2),
                dma(nz), dma(nz), dma(nz), dma(nz),
                pltpu.SemaphoreType.REGULAR((2,)),
            ],
            compiler_params=pltpu.CompilerParams(
                collective_id=0, has_side_effects=True, vmem_limit_bytes=60 * 1024 * 1024
            ),
        )(
            fields.reshape(2560, 128), joule_heat.reshape(512, 128), metric, diffusivity,
            face_flip, coarse_decay.reshape(8, 128),
        )
        advanced, pressure = pl.pallas_call(
            finish,
            name="finish",
            out_shape=(fields_shape, node_shape),
            in_specs=[anywhere] * 3,
            out_specs=(anywhere, anywhere),
            scratch_shapes=[vmem(2560, 128), vmem(512, 128), vmem(8, 128), dma(13)],
            compiler_params=pltpu.CompilerParams(vmem_limit_bytes=60 * 1024 * 1024),
        )(advanced, guess, back)
        return advanced.reshape(5, 512, 1, 128), pressure.reshape(512, 1, 128)

    in_specs = (
        P(None, None, ("slab", "sub"), None),
        P(None, ("slab", "sub"), None),
        P(),
        P(None, ("slab", "sub"), None),
        P(("slab", "sub")),
        P(None, ("slab", "sub"), None),
    )
    out_specs = (P(None, None, ("slab", "sub"), None), P(None, ("slab", "sub"), None))
    return jax.shard_map(local, mesh=mesh, in_specs=in_specs, out_specs=out_specs, check_vma=False)
```

```python
import functools

import jax
import jax.numpy as jnp
import numpy as np
from jax import lax
from jax.experimental import pallas as pl
from jax.experimental.pallas import tpu as pltpu
from jax.sharding import PartitionSpec as P

MESH = pl.DeviceIdType.MESH
CHUNKS = 5
F32 = jnp.float32

POINTS = np.cos(np.pi * np.arange(8) / 7.0)


def derivative():
    endings = np.ones(8)
    endings[0] = endings[7] = 2.0
    weighted = endings * (-1.0) ** np.arange(8)
    spacing = POINTS[:, None] - POINTS[None, :] + np.eye(8)
    derive = weighted[:, None] / weighted[None, :] / spacing
    return derive - np.eye(8) * np.sum(derive, axis=1)[:, None]


D = derivative()
K = D.T @ D
COLUMN_SQ = np.sum(D * D, axis=0)
H = np.stack([(1.0 - POINTS) / 2.0, (1.0 + POINTS) / 2.0])


def half_tables(matrix):
    even = (matrix[:4, :4] + matrix[:4, :3:-1]) / 2.0
    odd = (matrix[:4, :4] - matrix[:4, :3:-1]) / 2.0
    return even.tolist(), odd.tolist()


D_EVEN, D_ODD = half_tables(D)
K_EVEN, K_ODD = half_tables(K)


def dot4(row, parts):
    total = row[0] * parts[0]
    for a in range(1, 4):
        total = total + row[a] * parts[a]
    return total


def split(x):
    return [x[a] + x[7 - a] for a in range(4)], [x[a] - x[7 - a] for a in range(4)]


def apply_d(even, odd, p):
    from_even, from_odd = dot4(D_EVEN[p], even), dot4(D_ODD[p], odd)
    return from_odd + from_even, from_odd - from_even


def apply_k(even, odd, p):
    from_even, from_odd = dot4(K_EVEN[p], even), dot4(K_ODD[p], odd)
    return from_even + from_odd, from_even - from_odd


def ring(n, d):
    return min(d, n - d)


def kernel(
    sizes, fields, heat, metric, diffusivity, flip, decay, adv_out, guess_out, back_out,
    f, q, met, dif, flp, dec, s, u, tt, dv, fg, res, wgt, proj,
    face_l, face_r, got_l, got_r, pface_l, pface_r, pgot_l, pgot_r,
    near_out, near, mine, partner, rates, edge, backs,
    y_stat, y_push, y_pre, x_stat, x_push, x_pre, z_all, z_back, z_push, z_pre,
    load_sem, out_sem, face_send, face_recv, pface_send, pface_recv, near_send, near_recv,
    pair_sem, rate_sem, swap_sem, edge_send, edge_recv, push_send, push_recv, stat_send, stat_recv,
    stat_tail_send, stat_tail_recv, push_tail_send, push_tail_recv, both_sem, heard,
):
    nz, nx, ny = sizes
    chips_n = nx * ny
    sub_n = 2 * chips_n
    total = nz * sub_n
    z, sub = lax.axis_index("slab"), lax.axis_index("sub")
    core = lax.rem(sub, 2)
    chip = lax.div(sub, 2)
    cx, cy = lax.div(chip, ny), lax.rem(chip, ny)
    here = z * sub_n + sub
    at_start, at_end = here == 0, here == total - 1
    side = 2 * core - 1

    def at(position):
        position = lax.rem(position + total, total)
        return (lax.div(position, sub_n), lax.rem(position, sub_n))

    other_core = (z, sub - side)
    before, after = at(here - 1), at(here + 1)
    outer, outer_two, inner_two = at(here + side), at(here + 2 * side), at(here - 2 * side)
    chip_at = z * chips_n + chip
    more_before, more_after = chip_at > 0, chip_at < nz * chips_n - 1
    has_outer = jnp.where(core == 0, more_before, more_after)
    has_inner = jnp.where(core == 0, more_after, more_before)
    by_distance = lambda n: sorted(range(1, n), key=lambda d: -ring(n, d))
    y_order, x_order, z_order = by_distance(ny), by_distance(nx), by_distance(nz)

    def shift(dx, dy, dz):
        px, py = lax.rem(cx + dx + nx, nx), lax.rem(cy + dy + ny, ny)
        return (lax.rem(z + dz + nz, nz), (px * ny + py) * 2 + core)

    y_peers = [shift(0, d, 0) for d in y_order]
    x_peers = [shift(d, 0, 0) for d in x_order]
    z_peers = [shift(0, 0, d) for d in z_order]

    def remote(src, dst, send_sem, recv_sem, device):
        return pltpu.make_async_remote_copy(
            src_ref=src, dst_ref=dst, send_sem=send_sem, recv_sem=recv_sem,
            device_id=device, device_id_type=MESH,
        )

    def send(*args):
        copy = remote(*args)
        copy.start()
        return copy

    def when(condition, action):
        if condition is None:
            action()
        else:
            pl.when(condition)(action)

    class Exchange:
        def __init__(self, parts):
            self.parts = [(sent, got, remote(*args)) for sent, got, args in parts]

        def start(self):
            for sent, _, copy in self.parts:
                when(sent, copy.start)

        def wait(self):
            for sent, got, copy in self.parts:
                when(got, copy.wait_recv)
                when(sent, copy.wait_send)

    def wait_bytes(ref, sem):
        pltpu.make_async_copy(ref, ref, sem).wait()

    def offsets(n, wanted):
        return sorted({d % n for d in wanted} - {0})

    near_x = offsets(nx, (1, 2, 3))
    near_y = offsets(ny, (1, 2, -1, -2))
    near_z = offsets(nz, (1, 2, -1, -2))
    z_back[...] = jnp.zeros((nz, 2, 8, 128), F32)
    barrier = pltpu.get_barrier_semaphore()
    targets = [other_core] + [shift(d, 0, 0) for d in near_x]
    targets += [shift(0, d, 0) for d in near_y] + [shift(0, 0, d) for d in near_z]
    for condition, device in ((has_outer, outer), (has_inner, inner_two)):

        @pl.when(condition)
        def _():
            pl.semaphore_signal(barrier, inc=1, device_id=device, device_id_type=MESH)

    for device in targets:
        pl.semaphore_signal(barrier, inc=1, device_id=device, device_id_type=MESH)
    def load(src, dst, rows, k):
        return pltpu.make_async_copy(src.at[rows], dst.at[rows], load_sem.at[k])

    loads = [
        pltpu.make_async_copy(decay, dec, load_sem.at[0]),
        pltpu.make_async_copy(metric, met, load_sem.at[1]),
        pltpu.make_async_copy(flip, flp, load_sem.at[2]),
        pltpu.make_async_copy(diffusivity, dif, load_sem.at[3]),
    ]
    loads += [load(fields, f, pl.ds(512 * n, 512), 4 + n) for n in range(3)]
    ends_of = [512 * n + at_plane for n in (3, 4) for at_plane in (0, 448)]
    loads += [load(fields, f, pl.ds(spot, 64), 7 + k) for k, spot in enumerate(ends_of)]
    later = [load(fields, f, pl.ds(512 * n + 64, 384), 8 + n) for n in (3, 4)]
    later.append(pltpu.make_async_copy(heat, q, load_sem.at[13]))
    for copy in loads + later:
        copy.start()

    second = [shift(0, d, 0) for d in offsets(ny, (2, -2))] + [shift(0, 0, d) for d in offsets(nz, (2, -2))]
    third = [shift(0, 0, d) for d in offsets(nz, (4, -4))]

    def pass_word(k, devices):
        for device in devices:
            pl.semaphore_signal(heard.at[k], inc=1, device_id=device, device_id_type=MESH)

    for copy in loads:
        copy.wait()

    row = lax.broadcasted_iota(jnp.int32, (8, 128), 0)
    zero = jnp.zeros((8, 128), F32)
    wall = jnp.where((row == 0) | (row == 7), 0.0, 1.0)
    turned = (zero + flp[0].astype(F32)) == 1.0
    m = [jnp.broadcast_to(met[d], (8, 128)) for d in range(3)]
    msq = [m[d] * m[d] for d in range(3)]

    def by_row(values):
        out = zero + float(values[7])
        for k in range(7):
            out = jnp.where(row == k, float(values[k]), out)
        return out

    def reverse(x):
        half = pltpu.roll(x, 4, 0)
        pairs = jnp.where(lax.rem(row, 4) < 2, pltpu.roll(half, 6, 0), pltpu.roll(half, 2, 0))
        return jnp.where(lax.rem(row, 2) == 0, pltpu.roll(pairs, 7, 0), pltpu.roll(pairs, 1, 0))

    def oriented(x):
        return jnp.where(turned, reverse(x), x)

    def tile(ref, base):
        return ref.at[pl.ds(pl.multiple_of(base, 8), 8), :]

    def strided(ref, base, k):
        return ref[pl.ds(base + k, 8, stride=8), :]

    def start_velocity(i):
        def line(j, carry):
            at_row = i * 64 + j * 8
            x = [tile(f, n * 512 + at_row)[...] for n in range(5)]
            lifting = 0.015 * x[3] - 0.0125 - 0.0125 * jnp.tanh(0.5 * x[4])
            for n in range(3):
                tile(s, n * 512 + at_row)[...] = x[n] + lifting if n == 1 else x[n]
                tile(u, n * 512 + at_row)[...] = 0.01 * m[n] * x[n]
            return carry

        lax.fori_loop(0, 8, line, 0, unroll=4)

    def start_scalars(i):
        def line(j, carry):
            at_row = i * 64 + j * 8
            warmth, bubbles = tile(f, 1536 + at_row)[...], tile(f, 2048 + at_row)[...]
            warm, share = 0.05 + 0.025 * jnp.tanh(warmth), 0.5 - 0.5 * jnp.tanh(0.5 * bubbles)
            heating = tile(q, at_row)[...] * warm * share
            tile(s, 1536 + at_row)[...] = warmth + heating
            tile(s, 2048 + at_row)[...] = bubbles + 0.2 * heating
            return carry

        lax.fori_loop(0, 8, line, 0, unroll=4)

    def step_planes(n, planes):
        rate = dif[n]
        c1, c2 = rate * msq[1], rate * msq[2]
        for slot, i in enumerate(planes):
            at_row = i * 64
            even, odd = split([strided(f, n * 512 + at_row, k) for k in range(8)])
            for p in range(4):
                slopes, bends = apply_d(even, odd, p), apply_k(even, odd, p)
                for k, slope, bend in zip((p, 7 - p), slopes, bends):
                    spot = 64 * slot + 8 * k
                    tt[spot : spot + 8, :] = strided(u, 1024 + at_row, k) * slope + c2 * bend
        for slot, i in enumerate(planes):
            at_row = i * 64
            base = n * 512 + at_row
            even, odd = split([tile(f, base + 8 * j)[...] for j in range(8)])
            for p in range(4):
                slopes, bends = apply_d(even, odd, p), apply_k(even, odd, p)
                for j, slope, bend in zip((p, 7 - p), slopes, bends):
                    gone = tile(u, 512 + at_row + 8 * j)[...] * slope + c1 * bend
                    gone = gone + strided(tt, 64 * slot, j)
                    tile(s, base + 8 * j)[...] = tile(s, base + 8 * j)[...] - gone

    def step_lines(n, pairs):
        c0 = dif[n] * msq[0]
        keep = jnp.where(zero + (n < 3).astype(F32) > 0.5, wall, 1.0)

        def line(j, carry):
            base = n * 512 + j * 8
            even, odd = split([tile(f, base + 64 * i)[...] for i in range(8)])
            for p in pairs:
                slopes, bends = apply_d(even, odd, p), apply_k(even, odd, p)
                for i, slope, bend in zip((p, 7 - p), slopes, bends):
                    gone = tile(u, i * 64 + j * 8)[...] * slope + c0 * bend
                    tile(s, base + 64 * i)[...] = keep * (tile(s, base + 64 * i)[...] - gone)
            return carry

        lax.fori_loop(0, 8, line, 0, unroll=4)

    def join_span(ref, base):
        low, high = tile(ref, base), tile(ref, base + 56)
        shared = 0.5 * (low[...] + pltpu.roll(high[...], 1, 1))
        low[...] = shared
        high[...] = pltpu.roll(shared, 127, 1)

    def stage_faces(n):
        for j in range(8):
            spot = n * 64 + 8 * j
            tile(face_l, spot)[...] = oriented(tile(s, n * 512 + 8 * j)[...])
            tile(face_r, spot)[...] = tile(s, n * 512 + 448 + 8 * j)[...]

    def each(low, high, body, unroll=1):
        def run(n, carry):
            body(n)
            return carry

        lax.fori_loop(low, high, run, 0, unroll=unroll)

    near_out[0:8, :] = dec[...]
    near_out[8:16, :] = zero + flp[0].astype(F32)

    for i in (0, 7):
        start_velocity(i)

    def velocity_faces(n):
        step_planes(n, (0, 7))
        step_lines(n, (0,))
        for i in (0, 7):
            join_span(s, n * 512 + i * 64)
        stage_faces(n)

    each(0, 2, velocity_faces)

    pl.semaphore_wait(barrier, len(targets) + 2 * has_outer.astype(jnp.int32))
    def chain_exchange(left, right, from_left, from_right, sems, k):
        ahead, behind = jnp.logical_not(at_end), jnp.logical_not(at_start)
        return Exchange([
            (behind, ahead, (left, from_right, sems[0].at[k], sems[1].at[k], before)),
            (ahead, behind, (right, from_left, sems[0].at[k + 1], sems[1].at[k + 1], after)),
        ])

    def face_exchange(n, count, k):
        rows = pl.ds(n * 64, count * 64)
        return chain_exchange(
            face_l.at[rows], face_r.at[rows], got_l.at[rows], got_r.at[rows], (face_send, face_recv), k
        )

    pass_word(0, second)
    nears = Exchange([
        (None, None, (near_out, near.at[0], near_send.at[0], near_recv.at[0], other_core)),
        (has_outer, has_outer, (near_out, near.at[1], near_send.at[1], near_recv.at[1], outer)),
        (has_outer, has_inner, (near_out, near.at[2], near_send.at[2], near_recv.at[2], outer_two)),
    ])
    nears.start()
    for condition, k in ((has_outer, 1), (has_inner, 2)):

        @pl.when(jnp.logical_not(condition))
        def _():
            near[k] = jnp.zeros((16, 128), F32)

    for n in range(2):
        face_exchange(n, 1, 2 * n).start()
    each(2, 3, velocity_faces)

    face_exchange(2, 1, 4).start()

    for copy in later:
        copy.wait()
    each(1, 7, start_velocity)

    def velocity_rest(n):
        def planes(t, carry):
            step_planes(n, (1 + 2 * t, 2 + 2 * t))
            return carry

        lax.fori_loop(0, 3, planes, 0)
        step_lines(n, (1, 2, 3))
        for i in range(1, 7):
            join_span(s, n * 512 + i * 64)

    each(0, 2, velocity_rest)
    pl.semaphore_wait(heard.at[0], len(second))
    pass_word(1, third)
    rates[core, cy + 1] = dec[...]
    for device in y_peers:
        send(dec, rates.at[core, cy + 1], rate_sem.at[0], rate_sem.at[1], device)
    each(2, 3, velocity_rest)

    across = msq[2] * by_row(COLUMN_SQ) + 1.0
    for a in range(4):
        for b in range(4):
            under = across + (float(COLUMN_SQ[a]) * msq[0] + float(COLUMN_SQ[b]) * msq[1])
            wgt[8 * (4 * a + b) : 8 * (4 * a + b) + 8, :] = 0.5 / under

    nears.wait()
    own_a, partner_a, outer_a, far_a = dec[...], near[0, 0:8, :], near[1, 0:8, :], near[2, 0:8, :]
    first_core = zero + core.astype(F32) < 0.5
    not_start = 1.0 - at_start.astype(F32)
    not_end = 1.0 - at_end.astype(F32)
    a_0, a_1 = jnp.where(first_core, own_a, partner_a), jnp.where(first_core, partner_a, own_a)
    a_m, a_p = jnp.where(first_core, outer_a, far_a), jnp.where(first_core, far_a, outer_a)
    chip_first = (z * chips_n + chip == 0).astype(F32)
    chip_last = (z * chips_n + chip == nz * chips_n - 1).astype(F32)

    def root(a):
        return jnp.sqrt((1.0 - a) * (1.0 + a))

    s_0, s_1 = root(a_0), root(a_1)
    s_m, s_p = (1.0 - chip_first) * root(a_m), (1.0 - chip_last) * root(a_p)
    a_m, a_p = (1.0 - chip_first) * a_m, (1.0 - chip_last) * a_p

    edge[0] = a_m
    edge[1] = a_p
    ends = ((cy == 0, 0, (1, 0)), (cy == ny - 1, 1, (0, ny + 1)))
    for is_end, k, place in ends:

        @pl.when(is_end)
        def _():
            rates[place] = edge[k]
            for device in y_peers:
                send(edge.at[k], rates.at[place], edge_send.at[k], edge_recv.at[k], device)

    ends_last = row < 4
    A_0, A_1 = jnp.where(ends_last, a_0, a_1), jnp.where(ends_last, a_1, a_p)
    R_0, R_1 = jnp.where(ends_last, a_m, a_0), jnp.where(ends_last, a_0, a_1)
    C_1 = jnp.where(ends_last, a_0 * s_1 * a_1, s_1)
    s_own = jnp.where(first_core, s_0, s_1)
    a_before, s_before = jnp.where(first_core, a_m, a_0), jnp.where(first_core, s_m, s_0)
    a_after, s_after = jnp.where(first_core, a_1, a_p), jnp.where(first_core, s_1, s_p)
    k_1 = jnp.where(ends_last, s_own, a_after * s_own)
    k_2 = jnp.where(ends_last, own_a * s_before, s_after)
    k_3 = jnp.where(ends_last, a_before * s_own * s_own, s_own * s_own)
    k_4 = jnp.where(ends_last, a_before * s_own * k_2 + s_before * s_before, 0.0)
    flip_after = jnp.where(first_core, near[0, 8:16, :], near[1, 8:16, :]) == 1.0

    for n in range(3):
        face_exchange(n, 1, 2 * n).wait()
    start_mask, end_mask = zero + not_start > 0.5, zero + not_end > 0.5

    def join_chain(n):
        for j in range(8):
            spot = n * 64 + 8 * j
            low, high = tile(s, n * 512 + 8 * j), tile(s, n * 512 + 448 + 8 * j)
            low[...] = jnp.where(start_mask, 0.5 * (low[...] + oriented(tile(got_l, spot)[...])), low[...])
            high[...] = jnp.where(end_mask, 0.5 * (high[...] + tile(got_r, spot)[...]), high[...])

    each(0, 3, join_chain)

    def divergence_planes(t):
        for slot in range(2):
            at_row = (2 * t + slot) * 64
            even, odd = split([strided(s, 1024 + at_row, k) for k in range(8)])
            for p in range(4):
                for k, slope in zip((p, 7 - p), apply_d(even, odd, p)):
                    spot = 64 * slot + 8 * k
                    tt[spot : spot + 8, :] = m[2] * slope
        for slot in range(2):
            at_row = (2 * t + slot) * 64
            even, odd = split([tile(s, 512 + at_row + 8 * j)[...] for j in range(8)])
            for p in range(4):
                for j, slope in zip((p, 7 - p), apply_d(even, odd, p)):
                    tile(dv, at_row + 8 * j)[...] = m[1] * slope + strided(tt, 64 * slot, j)

    each(0, 4, divergence_planes)

    def guess_line(j):
        even, odd = split([tile(s, 64 * i + 8 * j)[...] for i in range(8)])
        nearer = jnp.minimum(j, 7 - j)
        for p in range(4):
            weight = tile(wgt, 8 * (4 * p + nearer))[...]
            for i, slope in zip((p, 7 - p), apply_d(even, odd, p)):
                spot = tile(dv, 64 * i + 8 * j)
                whole = spot[...] + m[0] * slope
                spot[...] = whole
                tile(fg, 64 * i + 8 * j)[...] = weight * whole

    each(0, 8, guess_line, 2)

    def residual_planes(t):
        for slot in range(2):
            at_row = (2 * t + slot) * 64
            even, odd = split([strided(fg, at_row, k) for k in range(8)])
            for p in range(4):
                for k, bend in zip((p, 7 - p), apply_k(even, odd, p)):
                    spot = 64 * slot + 8 * k
                    tt[spot : spot + 8, :] = msq[2] * bend
        for slot in range(2):
            at_row = (2 * t + slot) * 64
            even, odd = split([tile(fg, at_row + 8 * j)[...] for j in range(8)])
            for p in range(4):
                for j, bend in zip((p, 7 - p), apply_k(even, odd, p)):
                    at_j = at_row + 8 * j
                    gone = tile(fg, at_j)[...] + msq[1] * bend + strided(tt, 64 * slot, j)
                    tile(res, at_j)[...] = tile(dv, at_j)[...] - gone

    each(0, 4, residual_planes)

    def project_line(j):
        even, odd = split([tile(fg, 64 * i + 8 * j)[...] for i in range(8)])
        left = [None] * 8
        for p in range(4):
            for i, bend in zip((p, 7 - p), apply_k(even, odd, p)):
                left[i] = tile(res, 64 * i + 8 * j)[...] - msq[0] * bend
        low = high = None
        for i in range(1, 7):
            low = float(H[0, i]) * left[i] + (0.0 if low is None else low)
            high = float(H[1, i]) * left[i] + (0.0 if high is None else high)
        for n, part in enumerate((low, high, left[7], left[0])):
            tile(proj, n * 64 + 8 * j)[...] = part

    each(0, 8, project_line, 4)

    gap = [by_row(H[0]), by_row(H[1])]
    sums = []
    for n in range(4):
        x = [proj[n * 64 + 8 * j : n * 64 + 8 * j + 8, :] for j in range(8)]
        shared = 0.5 * (x[0] + pltpu.roll(x[7], 1, 1))
        x[0], x[7] = shared, pltpu.roll(shared, 127, 1)
        modes = []
        for b in range(2):
            part = None
            for j in range(8):
                if H[b, j] != 0.0:
                    part = float(H[b, j]) * x[j] + (0.0 if part is None else part)
            for e in range(2):
                modes.append(jnp.sum(part * gap[e], axis=0, keepdims=True) * (1.0 / 64.0))
        sums.append(modes)

    def rows_of(values):
        out = zero
        for k, value in enumerate(values):
            out = jnp.where(row == k, value, out)
        return out

    inside = rows_of(sums[0] + sums[1])
    on_face = rows_of(sums[2] + sums[3])
    across_face = rows_of(sums[3] + sums[2])
    swapped = rows_of([part[e] for part in (sums[3], sums[2]) for e in (1, 0, 3, 2)])
    swap = jnp.where(ends_last, turned.astype(F32), flip_after.astype(F32)) > 0.5
    pushed = 0.5 * jnp.where(swap, swapped, across_face)
    own_share = jnp.where(ends_last, 1.0 - 0.5 * not_end, 1.0 - 0.5 * not_start)
    rhs = inside + own_share * on_face

    b_own = k_1 * rhs + k_2 * pushed
    d_own = k_3 * rhs + k_4 * pushed
    mine[0] = b_own
    mine[1] = d_own
    pair = send(mine, partner, pair_sem.at[0], pair_sem.at[1], other_core)
    pair.wait()
    B_0, D_0 = jnp.where(first_core, b_own, partner[0]), jnp.where(first_core, d_own, partner[1])
    B_1, D_1 = jnp.where(first_core, partner[0], b_own), jnp.where(first_core, partner[1], d_own)
    y_push[cy, 0] = A_1 * B_0 + B_1
    y_push[cy, 1] = D_0 + R_0 * (C_1 * B_0 + D_1)

    def spread(ref, place, k, sems, devices):
        for device in devices:
            send(ref.at[place], ref.at[place], sems[0].at[k], sems[1].at[k], device)

    def spread_ended(ref, k, sem, devices):
        wait_bytes(ref.at[0 : len(devices)], sem.at[k])

    pushes, stats = (push_send, push_recv), (stat_send, stat_recv)
    def spread_z(ref, first, sems, k, tail_sems):
        rest = pl.ds(first, ref.shape[1] - first)
        for d, device in zip(z_order, z_peers):
            head = ref.at[z, pl.ds(0, first)]
            send(head, head, sems[0].at[k], sems[1].at[k], device)

            @pl.when(z + d >= nz)
            def _():
                tail = ref.at[z, rest]
                send(tail, tail, tail_sems[0].at[d], tail_sems[1].at[z], device)

    def spread_z_got(ref, first, sem, k, tail_sem):
        rest = pl.ds(first, ref.shape[1] - first)
        wait_bytes(ref.at[0 : nz - 1, pl.ds(0, first)], sem.at[k])
        for n in range(1, nz):

            @pl.when(z < n)
            def _():
                wait_bytes(ref.at[n, rest], tail_sem.at[n])

    def spread_z_left(ref, first, sem, k, tail_sem):
        rest = pl.ds(first, ref.shape[1] - first)
        wait_bytes(ref.at[0 : nz - 1, pl.ds(0, first)], sem.at[k])
        for d in range(1, nz):

            @pl.when(z + d >= nz)
            def _():
                wait_bytes(ref.at[z, rest], tail_sem.at[d])

    z_push_tail = (push_tail_send, push_tail_recv)
    spread(y_push, cy, 0, pushes, y_peers)

    wait_bytes(rates.at[core, pl.ds(1, ny - 1)], rate_sem.at[1])
    half = rates.at[core, pl.ds(1, ny)]
    swap_halves = send(half, half, swap_sem.at[0], swap_sem.at[1], other_core)
    for is_end, k, place in ends:

        @pl.when(jnp.logical_not(is_end))
        def _():
            wait_bytes(rates.at[place], edge_recv.at[k])

    swap_halves.wait()

    roots = [[root(rates[c, n + 1]) for n in range(ny)] for c in range(2)]
    for n in range(ny):
        e_m, e_0 = rates[1, n], rates[0, n + 1]
        e_1, e_p = rates[1, n + 1], rates[0, n + 2]
        both, lead = e_0 * e_1, e_m * e_0
        mixed = roots[0][n] + both * roots[1][n]
        y_stat[n, 0] = jnp.where(ends_last, both, e_1 * e_p)
        y_stat[n, 1] = jnp.where(ends_last, lead, both)
        y_stat[n, 2] = jnp.where(ends_last, lead * mixed, mixed)

    ones = zero + 1.0

    def combine_stat(stat, pre, count):
        up = ones
        for n in range(count):
            pre[n, 0] = up
            up = stat[n, 0] * up
        down, mixed = ones, zero
        for n in range(count - 1, -1, -1):
            pre[n, 1] = down
            pre[n, 2] = mixed
            mixed = stat[n, 1] * mixed + stat[n, 2] * pre[n, 0]
            down = stat[n, 1] * down
        return up, down, mixed

    def combine_push(stat, push, pre, count):
        up = zero
        for n in range(count):
            pre[n, 3] = up
            up = stat[n, 0] * up + push[n, 0]
        down = zero
        for n in range(count - 1, -1, -1):
            pre[n, 4] = down
            down = stat[n, 1] * down + (stat[n, 2] * pre[n, 3] + push[n, 1])
        return up, down

    def set_stat(ref, place, values):
        for k, value in enumerate(values):
            ref[place, k] = value

    set_stat(x_stat, cx, combine_stat(y_stat, y_pre, ny))
    spread(x_stat, cx, 0, stats, x_peers)

    each(0, 8, start_scalars)

    def scalars(n):
        def planes(t, carry):
            step_planes(n, (2 * t, 2 * t + 1))
            return carry

        lax.fori_loop(0, 4, planes, 0)
        step_lines(n, (0, 1, 2, 3))
        for i in range(8):
            join_span(s, n * 512 + i * 64)
        stage_faces(n)

    each(3, 5, scalars)
    for i in range(8):
        join_span(fg, 64 * i)
    for j in range(8):
        tile(pface_l, 8 * j)[...] = oriented(tile(fg, 8 * j)[...])
        tile(pface_r, 8 * j)[...] = tile(fg, 448 + 8 * j)[...]

    spread_ended(y_push, 0, push_recv, y_peers)
    set_stat(x_push, cx, combine_push(y_stat, y_push, y_pre, ny))
    spread(x_push, cx, 1, pushes, x_peers)
    pl.semaphore_wait(heard.at[1], len(third)) if third else None
    spread_ended(x_stat, 0, stat_recv, x_peers)
    slab_a, slab_r, slab_c = combine_stat(x_stat, x_pre, nx)

    @pl.when(core == 0)
    def _():
        z_all[z] = slab_a
        for device in z_peers:
            send(z_all.at[z], z_all.at[z], stat_send.at[1], stat_recv.at[1], device)

    @pl.when(core == 1)
    def _():
        z_back[z, 0] = slab_r
        z_back[z, 1] = slab_c

    for d, device in zip(z_order, z_peers):

        @pl.when((core == 1) & (z + d >= nz))
        def _():
            send(z_back.at[z], z_back.at[z], stat_tail_send.at[d], stat_tail_recv.at[z], device)


    guess_exchange = chain_exchange(pface_l, pface_r, pgot_l, pgot_r, (pface_send, pface_recv), 0)
    guess_exchange.start()
    face_exchange(3, 2, 6).start()
    spread_ended(x_push, 1, push_recv, x_peers)
    set_stat(z_push, z, combine_push(x_stat, x_push, x_pre, nx))
    spread_z(z_push, 1, pushes, 2, z_push_tail)
    wait_bytes(rates.at[core, pl.ds(1, ny - 1)], rate_sem.at[0])
    spread_ended(y_push, 0, push_send, y_peers)
    spread_ended(x_stat, 0, stat_send, x_peers)
    spread_ended(x_push, 1, push_send, x_peers)
    for is_end, k, place in ends:

        @pl.when(is_end)
        def _():
            wait_bytes(rates.at[0, pl.ds(1, ny - 1)], edge_send.at[k])

    guess_exchange.wait()
    for j in range(8):
        low, high = tile(fg, 8 * j), tile(fg, 448 + 8 * j)
        low[...] = jnp.where(start_mask, 0.5 * (low[...] + oriented(tile(pgot_l, 8 * j)[...])), low[...])
        high[...] = jnp.where(end_mask, 0.5 * (high[...] + tile(pgot_r, 8 * j)[...]), high[...])
    face_exchange(3, 2, 6).wait()
    each(3, 5, join_chain)
    adv_copy = pltpu.make_async_copy(s, adv_out, out_sem.at[0])
    adv_copy.start()

    guess_copy = pltpu.make_async_copy(fg, guess_out, out_sem.at[1])
    guess_copy.start()

    all_share = remote(z_all, z_all, both_sem.at[0], both_sem.at[1], other_core)
    back_share = remote(z_back, z_back, both_sem.at[2], both_sem.at[3], other_core)
    for n in range(1, nz):

        @pl.when((core == 1) & (z < n))
        def _():
            wait_bytes(z_back.at[n], stat_tail_recv.at[n])

    @pl.when(core == 1)
    def _():
        back_share.start()
        all_share.wait_recv()
        back_share.wait_send()

    @pl.when(core == 0)
    def _():
        wait_bytes(z_all.at[0 : nz - 1], stat_recv.at[1])
        all_share.start()
        back_share.wait_recv()
        all_share.wait_send()

    spread_z_got(z_push, 1, push_recv, 2, push_tail_recv)

    up = zero
    for n in range(nz):
        z_pre[n, 3] = up
        up = z_all[n] * up + z_push[n, 0]
    down = zero
    for n in range(nz - 1, -1, -1):
        further = z_back[n, 0] * down + (z_back[n, 1] * z_pre[n, 3] + z_push[n, 1])
        down = jnp.where(zero + (n > z).astype(F32) > 0.5, further, zero)
        z_pre[n, 4] = down
    up = z_pre[z, 3]
    down = z_pre[lax.rem(z + 1, nz), 4]
    down = jnp.where(zero + (z + 1 < nz).astype(F32) > 0.5, down, zero)
    for pre, place in ((x_pre, cx), (y_pre, cy)):
        down = pre[place, 4] + pre[place, 1] * down + pre[place, 2] * up
        up = pre[place, 3] + pre[place, 0] * up
    chip_up, chip_down = up, down
    middle = A_0 * chip_up + B_0
    up = jnp.where(first_core, chip_up, middle)
    down = jnp.where(first_core, R_1 * chip_down + C_1 * middle + D_1, chip_down)
    back = jnp.where(
        ends_last, down + s_own * (own_a * up + b_own), own_a * down + s_own * (up + s_own * rhs)
    )

    backs[...] = back
    back_copy = pltpu.make_async_copy(backs, back_out, out_sem.at[2])
    back_copy.start()

    @pl.when(core == 0)
    def _():
        wait_bytes(z_all.at[0 : nz - 1], stat_send.at[1])

    for d in range(1, nz):

        @pl.when((core == 1) & (z + d >= nz))
        def _():
            wait_bytes(z_back.at[z], stat_tail_send.at[d])

    spread_z_left(z_push, 1, push_send, 2, push_tail_send)
    adv_copy.wait()
    guess_copy.wait()
    back_copy.wait()


def finish(adv, guess, back, adv_out, prs_out, whole, fg, bk, sem):
    loads = [
        pltpu.make_async_copy(back, bk, sem.at[0]),
        pltpu.make_async_copy(guess, fg, sem.at[1]),
    ]
    come, go = [], []
    for n in range(CHUNKS):
        spot = pl.ds(n * (2560 // CHUNKS), 2560 // CHUNKS)
        come.append(pltpu.make_async_copy(adv.at[spot], whole.at[spot], sem.at[3 + n]))
        go.append(pltpu.make_async_copy(whole.at[spot], adv_out.at[spot], sem.at[3 + CHUNKS + n]))
    for copy in loads + come:
        copy.start()
    row = lax.broadcasted_iota(jnp.int32, (8, 128), 0)
    gap = []
    for b in range(2):
        values = jnp.full((8, 128), float(H[b, 7]), F32)
        for k in range(7):
            values = jnp.where(row == k, float(H[b, k]), values)
        gap.append(values)
    for copy in loads:
        copy.wait()
    modes = [jnp.broadcast_to(bk[k : k + 1, :], (8, 128)) for k in range(8)]
    edges = [gap[0] * modes[2 * k] + gap[1] * modes[2 * k + 1] for k in range(4)]
    for j in range(8):
        rims = [float(H[0, j]) * edges[2 * a] + float(H[1, j]) * edges[2 * a + 1] for a in range(2)]
        for i in range(8):
            at_ij = 64 * i + 8 * j
            guessed = fg[at_ij : at_ij + 8, :]
            fg[at_ij : at_ij + 8, :] = guessed + float(H[0, i]) * rims[0] + float(H[1, i]) * rims[1]
    out = pltpu.make_async_copy(fg, prs_out, sem.at[2])
    out.start()
    for n in range(CHUNKS):
        come[n].wait()
        go[n].start()
    for copy in go:
        copy.wait()
    out.wait()


def solution(mesh):
    nz, sub_n = mesh.shape["slab"], mesh.shape["sub"]
    nx = 2 if sub_n == 8 else 4
    ny = sub_n // (2 * nx)
    vmem = lambda *shape: pltpu.VMEM(shape, F32)
    dma = lambda n: pltpu.SemaphoreType.DMA((n,))
    anywhere = pl.BlockSpec(memory_space=pl.ANY)

    def local(fields, metric, diffusivity, joule_heat, face_flip, coarse_decay):
        fields_shape = jax.ShapeDtypeStruct((2560, 128), F32)
        node_shape = jax.ShapeDtypeStruct((512, 128), F32)
        mode_shape = jax.ShapeDtypeStruct((8, 128), F32)
        advanced, guess, back = pl.pallas_call(
            functools.partial(kernel, (nz, nx, ny)),
            name="step",
            out_shape=(fields_shape, node_shape, mode_shape),
            in_specs=[anywhere] * 6,
            out_specs=(anywhere, anywhere, anywhere),
            scratch_shapes=[
                vmem(2560, 128),
                vmem(512, 128),
                vmem(3, 1, 128),
                pltpu.SMEM((5,), F32),
                pltpu.SMEM((1,), jnp.int32),
                vmem(8, 128),
                vmem(2560, 128),
                vmem(1536, 128),
                vmem(128, 128),
                vmem(512, 128),
                vmem(512, 128),
                vmem(512, 128),
                vmem(128, 128),
                vmem(256, 128),
                vmem(320, 128),
                vmem(320, 128),
                vmem(320, 128),
                vmem(320, 128),
                vmem(64, 128),
                vmem(64, 128),
                vmem(64, 128),
                vmem(64, 128),
                vmem(16, 128),
                vmem(3, 16, 128),
                vmem(2, 8, 128),
                vmem(2, 8, 128),
                vmem(2, ny + 2, 8, 128),
                vmem(2, 8, 128),
                vmem(8, 128),
                vmem(ny, 3, 8, 128), vmem(ny, 2, 8, 128), vmem(ny, 5, 8, 128),
                vmem(nx, 3, 8, 128), vmem(nx, 2, 8, 128), vmem(nx, 5, 8, 128),
                vmem(nz, 8, 128), vmem(nz, 2, 8, 128), vmem(nz, 2, 8, 128), vmem(nz, 5, 8, 128),
                dma(14), dma(3), dma(8), dma(8), dma(2), dma(2), dma(3), dma(3),
                dma(2), dma(2), dma(2), dma(2), dma(2), dma(3), dma(3), dma(2), dma(2),
                dma(nz), dma(nz), dma(nz), dma(nz), dma(4),
                pltpu.SemaphoreType.REGULAR((2,)),
            ],
            compiler_params=pltpu.CompilerParams(
                collective_id=0, has_side_effects=True, vmem_limit_bytes=60 * 1024 * 1024
            ),
        )(
            fields.reshape(2560, 128), joule_heat.reshape(512, 128), metric, diffusivity,
            face_flip, coarse_decay.reshape(8, 128),
        )
        advanced, pressure = pl.pallas_call(
            finish,
            name="finish",
            out_shape=(fields_shape, node_shape),
            in_specs=[anywhere] * 3,
            out_specs=(anywhere, anywhere),
            scratch_shapes=[vmem(2560, 128), vmem(512, 128), vmem(8, 128), dma(3 + 2 * CHUNKS)],
            compiler_params=pltpu.CompilerParams(vmem_limit_bytes=60 * 1024 * 1024),
        )(advanced, guess, back)
        return advanced.reshape(5, 512, 1, 128), pressure.reshape(512, 1, 128)

    in_specs = (
        P(None, None, ("slab", "sub"), None),
        P(None, ("slab", "sub"), None),
        P(),
        P(None, ("slab", "sub"), None),
        P(("slab", "sub")),
        P(None, ("slab", "sub"), None),
    )
    out_specs = (P(None, None, ("slab", "sub"), None), P(None, ("slab", "sub"), None))
    return jax.shard_map(local, mesh=mesh, in_specs=in_specs, out_specs=out_specs, check_vma=False)
```

```python
import functools

import jax
import jax.numpy as jnp
import numpy as np
from jax import lax
from jax.experimental import pallas as pl
from jax.experimental.pallas import tpu as pltpu
from jax.sharding import PartitionSpec as P

MESH = pl.DeviceIdType.MESH
F32 = jnp.float32

POINTS = np.cos(np.pi * np.arange(8) / 7.0)


def derivative():
    endings = np.ones(8)
    endings[0] = endings[7] = 2.0
    weighted = endings * (-1.0) ** np.arange(8)
    spacing = POINTS[:, None] - POINTS[None, :] + np.eye(8)
    derive = weighted[:, None] / weighted[None, :] / spacing
    return derive - np.eye(8) * np.sum(derive, axis=1)[:, None]


D = derivative()
K = D.T @ D
COLUMN_SQ = np.sum(D * D, axis=0)
H = np.stack([(1.0 - POINTS) / 2.0, (1.0 + POINTS) / 2.0])


def half_tables(matrix):
    even = (matrix[:4, :4] + matrix[:4, :3:-1]) / 2.0
    odd = (matrix[:4, :4] - matrix[:4, :3:-1]) / 2.0
    return even.tolist(), odd.tolist()


D_EVEN, D_ODD = half_tables(D)
K_EVEN, K_ODD = half_tables(K)


def dot4(row, parts):
    total = row[0] * parts[0]
    for a in range(1, 4):
        total = total + row[a] * parts[a]
    return total


def split(x):
    return [x[a] + x[7 - a] for a in range(4)], [x[a] - x[7 - a] for a in range(4)]


def apply_d(even, odd, p):
    from_even, from_odd = dot4(D_EVEN[p], even), dot4(D_ODD[p], odd)
    return from_odd + from_even, from_odd - from_even


def apply_k(even, odd, p):
    from_even, from_odd = dot4(K_EVEN[p], even), dot4(K_ODD[p], odd)
    return from_even + from_odd, from_even - from_odd


def ring(n, d):
    return min(d, n - d)


def kernel(
    sizes, fields, heat, metric, diffusivity, flip, decay, s, fg, backs,
    f, q, met, dif, flp, dec, u, tt, dv, res, wgt, proj,
    face_l, face_r, got_l, got_r, pface_l, pface_r, pgot_l, pgot_r,
    near_out, near, mine, partner, rates, edge,
    y_stat, y_push, y_pre, x_stat, x_push, x_pre, z_all, z_back, z_push, z_pre,
    load_sem, face_send, face_recv, pface_send, pface_recv, near_send, near_recv,
    pair_sem, rate_sem, swap_sem, edge_send, edge_recv, push_send, push_recv, stat_send, stat_recv,
    stat_tail_send, stat_tail_recv, push_tail_send, push_tail_recv, both_sem, heard,
):
    nz, nx, ny = sizes
    chips_n = nx * ny
    sub_n = 2 * chips_n
    total = nz * sub_n
    z, sub = lax.axis_index("slab"), lax.axis_index("sub")
    core = lax.rem(sub, 2)
    chip = lax.div(sub, 2)
    cx, cy = lax.div(chip, ny), lax.rem(chip, ny)
    here = z * sub_n + sub
    at_start, at_end = here == 0, here == total - 1
    side = 2 * core - 1

    def at(position):
        position = lax.rem(position + total, total)
        return (lax.div(position, sub_n), lax.rem(position, sub_n))

    other_core = (z, sub - side)
    before, after = at(here - 1), at(here + 1)
    outer, outer_two, inner_two = at(here + side), at(here + 2 * side), at(here - 2 * side)
    chip_at = z * chips_n + chip
    more_before, more_after = chip_at > 0, chip_at < nz * chips_n - 1
    has_outer = jnp.where(core == 0, more_before, more_after)
    has_inner = jnp.where(core == 0, more_after, more_before)
    by_distance = lambda n: sorted(range(1, n), key=lambda d: -ring(n, d))
    y_order, x_order, z_order = by_distance(ny), by_distance(nx), by_distance(nz)

    def shift(dx, dy, dz):
        px, py = lax.rem(cx + dx + nx, nx), lax.rem(cy + dy + ny, ny)
        return (lax.rem(z + dz + nz, nz), (px * ny + py) * 2 + core)

    y_peers = [shift(0, d, 0) for d in y_order]
    x_peers = [shift(d, 0, 0) for d in x_order]
    z_peers = [shift(0, 0, d) for d in z_order]

    def remote(src, dst, send_sem, recv_sem, device):
        return pltpu.make_async_remote_copy(
            src_ref=src, dst_ref=dst, send_sem=send_sem, recv_sem=recv_sem,
            device_id=device, device_id_type=MESH,
        )

    def send(*args):
        copy = remote(*args)
        copy.start()
        return copy

    def when(condition, action):
        if condition is None:
            action()
        else:
            pl.when(condition)(action)

    class Exchange:
        def __init__(self, parts):
            self.parts = [(sent, got, remote(*args)) for sent, got, args in parts]

        def start(self):
            for sent, _, copy in self.parts:
                when(sent, copy.start)

        def wait(self):
            for sent, got, copy in self.parts:
                when(got, copy.wait_recv)
                when(sent, copy.wait_send)

    def wait_bytes(ref, sem):
        pltpu.make_async_copy(ref, ref, sem).wait()

    def offsets(n, wanted):
        return sorted({d % n for d in wanted} - {0})

    near_x = offsets(nx, (1, 2, 3))
    near_y = offsets(ny, (1, 2, -1, -2))
    near_z = offsets(nz, (1, 2, -1, -2))
    z_back[...] = jnp.zeros((nz, 2, 8, 128), F32)
    barrier = pltpu.get_barrier_semaphore()
    targets = [other_core] + [shift(d, 0, 0) for d in near_x]
    targets += [shift(0, d, 0) for d in near_y] + [shift(0, 0, d) for d in near_z]
    for condition, device in ((has_outer, outer), (has_inner, inner_two)):

        @pl.when(condition)
        def _():
            pl.semaphore_signal(barrier, inc=1, device_id=device, device_id_type=MESH)

    for device in targets:
        pl.semaphore_signal(barrier, inc=1, device_id=device, device_id_type=MESH)
    def load(src, dst, rows, k):
        return pltpu.make_async_copy(src.at[rows], dst.at[rows], load_sem.at[k])

    loads = [
        pltpu.make_async_copy(decay, dec, load_sem.at[0]),
        pltpu.make_async_copy(metric, met, load_sem.at[1]),
        pltpu.make_async_copy(flip, flp, load_sem.at[2]),
        pltpu.make_async_copy(diffusivity, dif, load_sem.at[3]),
    ]
    loads += [load(fields, f, pl.ds(512 * n, 512), 4 + n) for n in range(3)]
    ends_of = [512 * n + at_plane for n in (3, 4) for at_plane in (0, 448)]
    loads += [load(fields, f, pl.ds(spot, 64), 7 + k) for k, spot in enumerate(ends_of)]
    later = [load(fields, f, pl.ds(512 * n + 64, 384), 8 + n) for n in (3, 4)]
    later.append(pltpu.make_async_copy(heat, q, load_sem.at[13]))
    for copy in loads:
        copy.start()

    second = [shift(0, d, 0) for d in offsets(ny, (2, -2))] + [shift(0, 0, d) for d in offsets(nz, (2, -2))]
    third = [shift(0, 0, d) for d in offsets(nz, (4, -4))]

    def pass_word(k, devices):
        for device in devices:
            pl.semaphore_signal(heard.at[k], inc=1, device_id=device, device_id_type=MESH)

    for copy in loads:
        copy.wait()
    for copy in later:
        copy.start()

    row = lax.broadcasted_iota(jnp.int32, (8, 128), 0)
    zero = jnp.zeros((8, 128), F32)
    wall = jnp.where((row == 0) | (row == 7), 0.0, 1.0)
    turned = (zero + flp[0].astype(F32)) == 1.0
    m = [jnp.broadcast_to(met[d], (8, 128)) for d in range(3)]
    msq = [m[d] * m[d] for d in range(3)]

    def by_row(values):
        out = zero + float(values[7])
        for k in range(7):
            out = jnp.where(row == k, float(values[k]), out)
        return out

    def reverse(x):
        half = pltpu.roll(x, 4, 0)
        pairs = jnp.where(lax.rem(row, 4) < 2, pltpu.roll(half, 6, 0), pltpu.roll(half, 2, 0))
        return jnp.where(lax.rem(row, 2) == 0, pltpu.roll(pairs, 7, 0), pltpu.roll(pairs, 1, 0))

    def oriented(x):
        return jnp.where(turned, reverse(x), x)

    def tile(ref, base):
        return ref.at[pl.ds(pl.multiple_of(base, 8), 8), :]

    def strided(ref, base, k):
        return ref[pl.ds(base + k, 8, stride=8), :]

    def start_velocity(i):
        def line(j, carry):
            at_row = i * 64 + j * 8
            x = [tile(f, n * 512 + at_row)[...] for n in range(5)]
            lifting = 0.015 * x[3] - 0.0125 - 0.0125 * jnp.tanh(0.5 * x[4])
            for n in range(3):
                tile(s, n * 512 + at_row)[...] = x[n] + lifting if n == 1 else x[n]
                tile(u, n * 512 + at_row)[...] = 0.01 * m[n] * x[n]
            return carry

        lax.fori_loop(0, 8, line, 0, unroll=4)

    def start_scalars(i):
        def line(j, carry):
            at_row = i * 64 + j * 8
            warmth, bubbles = tile(f, 1536 + at_row)[...], tile(f, 2048 + at_row)[...]
            warm, share = 0.05 + 0.025 * jnp.tanh(warmth), 0.5 - 0.5 * jnp.tanh(0.5 * bubbles)
            heating = tile(q, at_row)[...] * warm * share
            tile(s, 1536 + at_row)[...] = warmth + heating
            tile(s, 2048 + at_row)[...] = bubbles + 0.2 * heating
            return carry

        lax.fori_loop(0, 8, line, 0, unroll=4)

    def step_planes(n, planes):
        rate = dif[n]
        c1, c2 = rate * msq[1], rate * msq[2]
        for slot, i in enumerate(planes):
            at_row = i * 64
            even, odd = split([strided(f, n * 512 + at_row, k) for k in range(8)])
            for p in range(4):
                slopes, bends = apply_d(even, odd, p), apply_k(even, odd, p)
                for k, slope, bend in zip((p, 7 - p), slopes, bends):
                    spot = 64 * slot + 8 * k
                    tt[spot : spot + 8, :] = strided(u, 1024 + at_row, k) * slope + c2 * bend
        for slot, i in enumerate(planes):
            at_row = i * 64
            base = n * 512 + at_row
            even, odd = split([tile(f, base + 8 * j)[...] for j in range(8)])
            for p in range(4):
                slopes, bends = apply_d(even, odd, p), apply_k(even, odd, p)
                for j, slope, bend in zip((p, 7 - p), slopes, bends):
                    gone = tile(u, 512 + at_row + 8 * j)[...] * slope + c1 * bend
                    gone = gone + strided(tt, 64 * slot, j)
                    tile(s, base + 8 * j)[...] = tile(s, base + 8 * j)[...] - gone

    def step_lines(n, pairs):
        c0 = dif[n] * msq[0]
        keep = jnp.where(zero + (n < 3).astype(F32) > 0.5, wall, 1.0)

        def line(j, carry):
            base = n * 512 + j * 8
            even, odd = split([tile(f, base + 64 * i)[...] for i in range(8)])
            for p in pairs:
                slopes, bends = apply_d(even, odd, p), apply_k(even, odd, p)
                for i, slope, bend in zip((p, 7 - p), slopes, bends):
                    gone = tile(u, i * 64 + j * 8)[...] * slope + c0 * bend
                    tile(s, base + 64 * i)[...] = keep * (tile(s, base + 64 * i)[...] - gone)
            return carry

        lax.fori_loop(0, 8, line, 0, unroll=4)

    def join_span(ref, base):
        low, high = tile(ref, base), tile(ref, base + 56)
        shared = 0.5 * (low[...] + pltpu.roll(high[...], 1, 1))
        low[...] = shared
        high[...] = pltpu.roll(shared, 127, 1)

    def stage_faces(n):
        for j in range(8):
            spot = n * 64 + 8 * j
            tile(face_l, spot)[...] = oriented(tile(s, n * 512 + 8 * j)[...])
            tile(face_r, spot)[...] = tile(s, n * 512 + 448 + 8 * j)[...]

    def each(low, high, body, unroll=1):
        def run(n, carry):
            body(n)
            return carry

        lax.fori_loop(low, high, run, 0, unroll=unroll)

    near_out[0:8, :] = dec[...]
    near_out[8:16, :] = zero + flp[0].astype(F32)

    for i in (0, 7):
        start_velocity(i)

    def velocity_faces(n):
        step_planes(n, (0, 7))
        step_lines(n, (0,))
        for i in (0, 7):
            join_span(s, n * 512 + i * 64)
        stage_faces(n)

    each(0, 3, velocity_faces)

    pl.semaphore_wait(barrier, len(targets) + 2 * has_outer.astype(jnp.int32))
    def chain_exchange(left, right, from_left, from_right, sems, k):
        ahead, behind = jnp.logical_not(at_end), jnp.logical_not(at_start)
        return Exchange([
            (behind, ahead, (left, from_right, sems[0].at[k], sems[1].at[k], before)),
            (ahead, behind, (right, from_left, sems[0].at[k + 1], sems[1].at[k + 1], after)),
        ])

    def face_exchange(n, count, k):
        rows = pl.ds(n * 64, count * 64)
        return chain_exchange(
            face_l.at[rows], face_r.at[rows], got_l.at[rows], got_r.at[rows], (face_send, face_recv), k
        )

    pass_word(0, second)
    nears = Exchange([
        (None, None, (near_out, near.at[0], near_send.at[0], near_recv.at[0], other_core)),
        (has_outer, has_outer, (near_out, near.at[1], near_send.at[1], near_recv.at[1], outer)),
        (has_outer, has_inner, (near_out, near.at[2], near_send.at[2], near_recv.at[2], outer_two)),
    ])
    nears.start()
    for condition, k in ((has_outer, 1), (has_inner, 2)):

        @pl.when(jnp.logical_not(condition))
        def _():
            near[k] = jnp.zeros((16, 128), F32)

    for n in range(3):
        face_exchange(n, 1, 2 * n).start()

    for copy in later:
        copy.wait()
    each(1, 7, start_velocity)

    def velocity_rest(n):
        def planes(t, carry):
            step_planes(n, (1 + 2 * t, 2 + 2 * t))
            return carry

        lax.fori_loop(0, 3, planes, 0)
        step_lines(n, (1, 2, 3))
        for i in range(1, 7):
            join_span(s, n * 512 + i * 64)

    each(0, 2, velocity_rest)
    pl.semaphore_wait(heard.at[0], len(second))
    pass_word(1, third)
    rates[core, cy + 1] = dec[...]
    for device in y_peers:
        send(dec, rates.at[core, cy + 1], rate_sem.at[0], rate_sem.at[1], device)
    each(2, 3, velocity_rest)

    across = msq[2] * by_row(COLUMN_SQ) + 1.0
    for a in range(4):
        for b in range(4):
            under = across + (float(COLUMN_SQ[a]) * msq[0] + float(COLUMN_SQ[b]) * msq[1])
            wgt[8 * (4 * a + b) : 8 * (4 * a + b) + 8, :] = 0.5 / under

    nears.wait()
    own_a, partner_a, outer_a, far_a = dec[...], near[0, 0:8, :], near[1, 0:8, :], near[2, 0:8, :]
    first_core = zero + core.astype(F32) < 0.5
    not_start = 1.0 - at_start.astype(F32)
    not_end = 1.0 - at_end.astype(F32)
    a_0, a_1 = jnp.where(first_core, own_a, partner_a), jnp.where(first_core, partner_a, own_a)
    a_m, a_p = jnp.where(first_core, outer_a, far_a), jnp.where(first_core, far_a, outer_a)
    chip_first = (z * chips_n + chip == 0).astype(F32)
    chip_last = (z * chips_n + chip == nz * chips_n - 1).astype(F32)

    def root(a):
        return jnp.sqrt((1.0 - a) * (1.0 + a))

    s_0, s_1 = root(a_0), root(a_1)
    s_m, s_p = (1.0 - chip_first) * root(a_m), (1.0 - chip_last) * root(a_p)
    a_m, a_p = (1.0 - chip_first) * a_m, (1.0 - chip_last) * a_p

    edge[0] = a_m
    edge[1] = a_p
    ends = ((cy == 0, 0, (1, 0)), (cy == ny - 1, 1, (0, ny + 1)))
    for is_end, k, place in ends:

        @pl.when(is_end)
        def _():
            rates[place] = edge[k]
            for device in y_peers:
                send(edge.at[k], rates.at[place], edge_send.at[k], edge_recv.at[k], device)

    ends_last = row < 4
    A_0, A_1 = jnp.where(ends_last, a_0, a_1), jnp.where(ends_last, a_1, a_p)
    R_0, R_1 = jnp.where(ends_last, a_m, a_0), jnp.where(ends_last, a_0, a_1)
    C_1 = jnp.where(ends_last, a_0 * s_1 * a_1, s_1)
    s_own = jnp.where(first_core, s_0, s_1)
    a_before, s_before = jnp.where(first_core, a_m, a_0), jnp.where(first_core, s_m, s_0)
    a_after, s_after = jnp.where(first_core, a_1, a_p), jnp.where(first_core, s_1, s_p)
    k_1 = jnp.where(ends_last, s_own, a_after * s_own)
    k_2 = jnp.where(ends_last, own_a * s_before, s_after)
    k_3 = jnp.where(ends_last, a_before * s_own * s_own, s_own * s_own)
    k_4 = jnp.where(ends_last, a_before * s_own * k_2 + s_before * s_before, 0.0)
    flip_after = jnp.where(first_core, near[0, 8:16, :], near[1, 8:16, :]) == 1.0

    for n in range(3):
        face_exchange(n, 1, 2 * n).wait()
    start_mask, end_mask = zero + not_start > 0.5, zero + not_end > 0.5

    def join_chain(n):
        for j in range(8):
            spot = n * 64 + 8 * j
            low, high = tile(s, n * 512 + 8 * j), tile(s, n * 512 + 448 + 8 * j)
            low[...] = jnp.where(start_mask, 0.5 * (low[...] + oriented(tile(got_l, spot)[...])), low[...])
            high[...] = jnp.where(end_mask, 0.5 * (high[...] + tile(got_r, spot)[...]), high[...])

    each(0, 3, join_chain)

    def divergence_planes(t):
        for slot in range(2):
            at_row = (2 * t + slot) * 64
            even, odd = split([strided(s, 1024 + at_row, k) for k in range(8)])
            for p in range(4):
                for k, slope in zip((p, 7 - p), apply_d(even, odd, p)):
                    spot = 64 * slot + 8 * k
                    tt[spot : spot + 8, :] = m[2] * slope
        for slot in range(2):
            at_row = (2 * t + slot) * 64
            even, odd = split([tile(s, 512 + at_row + 8 * j)[...] for j in range(8)])
            for p in range(4):
                for j, slope in zip((p, 7 - p), apply_d(even, odd, p)):
                    tile(dv, at_row + 8 * j)[...] = m[1] * slope + strided(tt, 64 * slot, j)

    each(0, 4, divergence_planes, 2)

    def guess_line(j):
        even, odd = split([tile(s, 64 * i + 8 * j)[...] for i in range(8)])
        nearer = jnp.minimum(j, 7 - j)
        for p in range(4):
            weight = tile(wgt, 8 * (4 * p + nearer))[...]
            for i, slope in zip((p, 7 - p), apply_d(even, odd, p)):
                spot = tile(dv, 64 * i + 8 * j)
                whole = spot[...] + m[0] * slope
                spot[...] = whole
                tile(fg, 64 * i + 8 * j)[...] = weight * whole

    each(0, 8, guess_line, 4)

    def residual_planes(t):
        for slot in range(2):
            at_row = (2 * t + slot) * 64
            even, odd = split([strided(fg, at_row, k) for k in range(8)])
            for p in range(4):
                for k, bend in zip((p, 7 - p), apply_k(even, odd, p)):
                    spot = 64 * slot + 8 * k
                    tt[spot : spot + 8, :] = msq[2] * bend
        for slot in range(2):
            at_row = (2 * t + slot) * 64
            even, odd = split([tile(fg, at_row + 8 * j)[...] for j in range(8)])
            for p in range(4):
                for j, bend in zip((p, 7 - p), apply_k(even, odd, p)):
                    at_j = at_row + 8 * j
                    gone = tile(fg, at_j)[...] + msq[1] * bend + strided(tt, 64 * slot, j)
                    tile(res, at_j)[...] = tile(dv, at_j)[...] - gone

    each(0, 4, residual_planes, 2)

    def project_line(j):
        even, odd = split([tile(fg, 64 * i + 8 * j)[...] for i in range(8)])
        left = [None] * 8
        for p in range(4):
            for i, bend in zip((p, 7 - p), apply_k(even, odd, p)):
                left[i] = tile(res, 64 * i + 8 * j)[...] - msq[0] * bend
        low = high = None
        for i in range(1, 7):
            low = float(H[0, i]) * left[i] + (0.0 if low is None else low)
            high = float(H[1, i]) * left[i] + (0.0 if high is None else high)
        for n, part in enumerate((low, high, left[7], left[0])):
            tile(proj, n * 64 + 8 * j)[...] = part

    each(0, 8, project_line, 8)

    gap = [by_row(H[0]), by_row(H[1])]
    sums = []
    for n in range(4):
        x = [proj[n * 64 + 8 * j : n * 64 + 8 * j + 8, :] for j in range(8)]
        shared = 0.5 * (x[0] + pltpu.roll(x[7], 1, 1))
        x[0], x[7] = shared, pltpu.roll(shared, 127, 1)
        modes = []
        for b in range(2):
            part = None
            for j in range(8):
                if H[b, j] != 0.0:
                    part = float(H[b, j]) * x[j] + (0.0 if part is None else part)
            for e in range(2):
                modes.append(jnp.sum(part * gap[e], axis=0, keepdims=True) * (1.0 / 64.0))
        sums.append(modes)

    def rows_of(values):
        out = zero
        for k, value in enumerate(values):
            out = jnp.where(row == k, value, out)
        return out

    inside = rows_of(sums[0] + sums[1])
    on_face = rows_of(sums[2] + sums[3])
    across_face = rows_of(sums[3] + sums[2])
    swapped = rows_of([part[e] for part in (sums[3], sums[2]) for e in (1, 0, 3, 2)])
    swap = jnp.where(ends_last, turned.astype(F32), flip_after.astype(F32)) > 0.5
    pushed = 0.5 * jnp.where(swap, swapped, across_face)
    own_share = jnp.where(ends_last, 1.0 - 0.5 * not_end, 1.0 - 0.5 * not_start)
    rhs = inside + own_share * on_face

    b_own = k_1 * rhs + k_2 * pushed
    d_own = k_3 * rhs + k_4 * pushed
    mine[0] = b_own
    mine[1] = d_own
    pair = send(mine, partner, pair_sem.at[0], pair_sem.at[1], other_core)
    pair.wait()
    B_0, D_0 = jnp.where(first_core, b_own, partner[0]), jnp.where(first_core, d_own, partner[1])
    B_1, D_1 = jnp.where(first_core, partner[0], b_own), jnp.where(first_core, partner[1], d_own)
    y_push[cy, 0] = A_1 * B_0 + B_1
    y_push[cy, 1] = D_0 + R_0 * (C_1 * B_0 + D_1)

    def spread(ref, place, k, sems, devices):
        for device in devices:
            send(ref.at[place], ref.at[place], sems[0].at[k], sems[1].at[k], device)

    def spread_ended(ref, k, sem, devices):
        wait_bytes(ref.at[0 : len(devices)], sem.at[k])

    pushes, stats = (push_send, push_recv), (stat_send, stat_recv)
    def spread_z(ref, first, sems, k, tail_sems):
        rest = pl.ds(first, ref.shape[1] - first)
        for d, device in zip(z_order, z_peers):
            head = ref.at[z, pl.ds(0, first)]
            send(head, head, sems[0].at[k], sems[1].at[k], device)

            @pl.when(z + d >= nz)
            def _():
                tail = ref.at[z, rest]
                send(tail, tail, tail_sems[0].at[d], tail_sems[1].at[z], device)

    def spread_z_got(ref, first, sem, k, tail_sem):
        rest = pl.ds(first, ref.shape[1] - first)
        wait_bytes(ref.at[0 : nz - 1, pl.ds(0, first)], sem.at[k])
        for n in range(1, nz):

            @pl.when(z < n)
            def _():
                wait_bytes(ref.at[n, rest], tail_sem.at[n])

    def spread_z_left(ref, first, sem, k, tail_sem):
        rest = pl.ds(first, ref.shape[1] - first)
        wait_bytes(ref.at[0 : nz - 1, pl.ds(0, first)], sem.at[k])
        for d in range(1, nz):

            @pl.when(z + d >= nz)
            def _():
                wait_bytes(ref.at[z, rest], tail_sem.at[d])

    z_push_tail = (push_tail_send, push_tail_recv)
    spread(y_push, cy, 0, pushes, y_peers)

    wait_bytes(rates.at[core, pl.ds(1, ny - 1)], rate_sem.at[1])
    half = rates.at[core, pl.ds(1, ny)]
    swap_halves = send(half, half, swap_sem.at[0], swap_sem.at[1], other_core)
    for is_end, k, place in ends:

        @pl.when(jnp.logical_not(is_end))
        def _():
            wait_bytes(rates.at[place], edge_recv.at[k])

    swap_halves.wait()

    roots = [[root(rates[c, n + 1]) for n in range(ny)] for c in range(2)]
    for n in range(ny):
        e_m, e_0 = rates[1, n], rates[0, n + 1]
        e_1, e_p = rates[1, n + 1], rates[0, n + 2]
        both, lead = e_0 * e_1, e_m * e_0
        mixed = roots[0][n] + both * roots[1][n]
        y_stat[n, 0] = jnp.where(ends_last, both, e_1 * e_p)
        y_stat[n, 1] = jnp.where(ends_last, lead, both)
        y_stat[n, 2] = jnp.where(ends_last, lead * mixed, mixed)

    ones = zero + 1.0

    def combine_stat(stat, pre, count):
        up = ones
        for n in range(count):
            pre[n, 0] = up
            up = stat[n, 0] * up
        down, mixed = ones, zero
        for n in range(count - 1, -1, -1):
            pre[n, 1] = down
            pre[n, 2] = mixed
            mixed = stat[n, 1] * mixed + stat[n, 2] * pre[n, 0]
            down = stat[n, 1] * down
        return up, down, mixed

    def combine_push(stat, push, pre, count):
        up = zero
        for n in range(count):
            pre[n, 3] = up
            up = stat[n, 0] * up + push[n, 0]
        down = zero
        for n in range(count - 1, -1, -1):
            pre[n, 4] = down
            down = stat[n, 1] * down + (stat[n, 2] * pre[n, 3] + push[n, 1])
        return up, down

    def set_stat(ref, place, values):
        for k, value in enumerate(values):
            ref[place, k] = value

    set_stat(x_stat, cx, combine_stat(y_stat, y_pre, ny))
    spread(x_stat, cx, 0, stats, x_peers)

    each(0, 8, start_scalars)

    def scalars(n):
        def planes(t, carry):
            step_planes(n, (2 * t, 2 * t + 1))
            return carry

        lax.fori_loop(0, 4, planes, 0)
        step_lines(n, (0, 1, 2, 3))
        for i in range(8):
            join_span(s, n * 512 + i * 64)
        stage_faces(n)

    each(3, 5, scalars)
    for i in range(8):
        join_span(fg, 64 * i)
    for j in range(8):
        tile(pface_l, 8 * j)[...] = oriented(tile(fg, 8 * j)[...])
        tile(pface_r, 8 * j)[...] = tile(fg, 448 + 8 * j)[...]

    spread_ended(y_push, 0, push_recv, y_peers)
    set_stat(x_push, cx, combine_push(y_stat, y_push, y_pre, ny))
    spread(x_push, cx, 1, pushes, x_peers)
    pl.semaphore_wait(heard.at[1], len(third)) if third else None
    spread_ended(x_stat, 0, stat_recv, x_peers)
    slab_a, slab_r, slab_c = combine_stat(x_stat, x_pre, nx)

    @pl.when(core == 0)
    def _():
        z_all[z] = slab_a
        for device in z_peers:
            send(z_all.at[z], z_all.at[z], stat_send.at[1], stat_recv.at[1], device)

    @pl.when(core == 1)
    def _():
        z_back[z, 0] = slab_r
        z_back[z, 1] = slab_c

    for d, device in zip(z_order, z_peers):

        @pl.when((core == 1) & (z + d >= nz))
        def _():
            send(z_back.at[z], z_back.at[z], stat_tail_send.at[d], stat_tail_recv.at[z], device)


    guess_exchange = chain_exchange(pface_l, pface_r, pgot_l, pgot_r, (pface_send, pface_recv), 0)
    guess_exchange.start()
    face_exchange(3, 2, 6).start()
    spread_ended(x_push, 1, push_recv, x_peers)
    set_stat(z_push, z, combine_push(x_stat, x_push, x_pre, nx))
    spread_z(z_push, 1, pushes, 2, z_push_tail)
    wait_bytes(rates.at[core, pl.ds(1, ny - 1)], rate_sem.at[0])
    spread_ended(y_push, 0, push_send, y_peers)
    spread_ended(x_stat, 0, stat_send, x_peers)
    spread_ended(x_push, 1, push_send, x_peers)
    for is_end, k, place in ends:

        @pl.when(is_end)
        def _():
            wait_bytes(rates.at[0, pl.ds(1, ny - 1)], edge_send.at[k])

    guess_exchange.wait()
    for j in range(8):
        low, high = tile(fg, 8 * j), tile(fg, 448 + 8 * j)
        low[...] = jnp.where(start_mask, 0.5 * (low[...] + oriented(tile(pgot_l, 8 * j)[...])), low[...])
        high[...] = jnp.where(end_mask, 0.5 * (high[...] + tile(pgot_r, 8 * j)[...]), high[...])
    face_exchange(3, 2, 6).wait()
    each(3, 5, join_chain)


    all_share = remote(z_all, z_all, both_sem.at[0], both_sem.at[1], other_core)
    back_share = remote(z_back, z_back, both_sem.at[2], both_sem.at[3], other_core)
    for n in range(1, nz):

        @pl.when((core == 1) & (z < n))
        def _():
            wait_bytes(z_back.at[n], stat_tail_recv.at[n])

    @pl.when(core == 1)
    def _():
        back_share.start()
        all_share.wait_recv()
        back_share.wait_send()

    @pl.when(core == 0)
    def _():
        wait_bytes(z_all.at[0 : nz - 1], stat_recv.at[1])
        all_share.start()
        back_share.wait_recv()
        all_share.wait_send()

    spread_z_got(z_push, 1, push_recv, 2, push_tail_recv)

    up = zero
    for n in range(nz):
        z_pre[n, 3] = up
        up = z_all[n] * up + z_push[n, 0]
    down = zero
    for n in range(nz - 1, -1, -1):
        further = z_back[n, 0] * down + (z_back[n, 1] * z_pre[n, 3] + z_push[n, 1])
        down = jnp.where(zero + (n > z).astype(F32) > 0.5, further, zero)
        z_pre[n, 4] = down
    up = z_pre[z, 3]
    down = z_pre[lax.rem(z + 1, nz), 4]
    down = jnp.where(zero + (z + 1 < nz).astype(F32) > 0.5, down, zero)
    for pre, place in ((x_pre, cx), (y_pre, cy)):
        down = pre[place, 4] + pre[place, 1] * down + pre[place, 2] * up
        up = pre[place, 3] + pre[place, 0] * up
    chip_up, chip_down = up, down
    middle = A_0 * chip_up + B_0
    up = jnp.where(first_core, chip_up, middle)
    down = jnp.where(first_core, R_1 * chip_down + C_1 * middle + D_1, chip_down)
    back = jnp.where(
        ends_last, down + s_own * (own_a * up + b_own), own_a * down + s_own * (up + s_own * rhs)
    )

    backs[...] = back

    @pl.when(core == 0)
    def _():
        wait_bytes(z_all.at[0 : nz - 1], stat_send.at[1])

    for d in range(1, nz):

        @pl.when((core == 1) & (z + d >= nz))
        def _():
            wait_bytes(z_back.at[z], stat_tail_send.at[d])

    spread_z_left(z_push, 1, push_send, 2, push_tail_send)


def finish(adv, guess, back, adv_out, prs_out, fg, sem):
    move = pltpu.make_async_copy(adv, adv_out, sem.at[0])
    move.start()
    row = lax.broadcasted_iota(jnp.int32, (8, 128), 0)
    gap = []
    for b in range(2):
        values = jnp.full((8, 128), float(H[b, 7]), F32)
        for k in range(7):
            values = jnp.where(row == k, float(H[b, k]), values)
        gap.append(values)
    modes = [jnp.broadcast_to(back[k : k + 1, :], (8, 128)) for k in range(8)]
    edges = [gap[0] * modes[2 * k] + gap[1] * modes[2 * k + 1] for k in range(4)]
    for j in range(8):
        rims = [float(H[0, j]) * edges[2 * a] + float(H[1, j]) * edges[2 * a + 1] for a in range(2)]
        for i in range(8):
            at_ij = 64 * i + 8 * j
            guessed = guess[at_ij : at_ij + 8, :]
            fg[at_ij : at_ij + 8, :] = guessed + float(H[0, i]) * rims[0] + float(H[1, i]) * rims[1]
    out = pltpu.make_async_copy(fg, prs_out, sem.at[1])
    out.start()
    move.wait()
    out.wait()


def solution(mesh):
    nz, sub_n = mesh.shape["slab"], mesh.shape["sub"]
    nx = 2 if sub_n == 8 else 4
    ny = sub_n // (2 * nx)
    vmem = lambda *shape: pltpu.VMEM(shape, F32)
    dma = lambda n: pltpu.SemaphoreType.DMA((n,))
    anywhere = pl.BlockSpec(memory_space=pl.ANY)
    inside = pl.BlockSpec(memory_space=pltpu.VMEM)

    def local(fields, metric, diffusivity, joule_heat, face_flip, coarse_decay):
        fields_shape = jax.ShapeDtypeStruct((2560, 128), F32)
        node_shape = jax.ShapeDtypeStruct((512, 128), F32)
        mode_shape = jax.ShapeDtypeStruct((8, 128), F32)
        advanced, guess, back = pl.pallas_call(
            functools.partial(kernel, (nz, nx, ny)),
            name="step",
            out_shape=(pltpu.VMEM((2560, 128), F32), pltpu.VMEM((512, 128), F32), pltpu.VMEM((8, 128), F32)),
            in_specs=[anywhere] * 6,
            out_specs=(inside, inside, inside),
            scratch_shapes=[
                vmem(2560, 128),
                vmem(512, 128),
                vmem(3, 1, 128),
                pltpu.SMEM((5,), F32),
                pltpu.SMEM((1,), jnp.int32),
                vmem(8, 128),
                vmem(1536, 128),
                vmem(128, 128),
                vmem(512, 128),
                vmem(512, 128),
                vmem(128, 128),
                vmem(256, 128),
                vmem(320, 128),
                vmem(320, 128),
                vmem(320, 128),
                vmem(320, 128),
                vmem(64, 128),
                vmem(64, 128),
                vmem(64, 128),
                vmem(64, 128),
                vmem(16, 128),
                vmem(3, 16, 128),
                vmem(2, 8, 128),
                vmem(2, 8, 128),
                vmem(2, ny + 2, 8, 128),
                vmem(2, 8, 128),
                vmem(ny, 3, 8, 128), vmem(ny, 2, 8, 128), vmem(ny, 5, 8, 128),
                vmem(nx, 3, 8, 128), vmem(nx, 2, 8, 128), vmem(nx, 5, 8, 128),
                vmem(nz, 8, 128), vmem(nz, 2, 8, 128), vmem(nz, 2, 8, 128), vmem(nz, 5, 8, 128),
                dma(14), dma(8), dma(8), dma(2), dma(2), dma(3), dma(3),
                dma(2), dma(2), dma(2), dma(2), dma(2), dma(3), dma(3), dma(2), dma(2),
                dma(nz), dma(nz), dma(nz), dma(nz), dma(4),
                pltpu.SemaphoreType.REGULAR((2,)),
            ],
            compiler_params=pltpu.CompilerParams(
                collective_id=0, has_side_effects=True, vmem_limit_bytes=60 * 1024 * 1024
            ),
        )(
            fields.reshape(2560, 128), joule_heat.reshape(512, 128), metric, diffusivity,
            face_flip, coarse_decay.reshape(8, 128),
        )
        advanced, pressure = pl.pallas_call(
            finish,
            name="finish",
            out_shape=(fields_shape, node_shape),
            in_specs=[inside] * 3,
            out_specs=(anywhere, anywhere),
            scratch_shapes=[vmem(512, 128), dma(2)],
            compiler_params=pltpu.CompilerParams(vmem_limit_bytes=16 * 1024 * 1024),
        )(advanced, guess, back)
        return advanced.reshape(5, 512, 1, 128), pressure.reshape(512, 1, 128)

    in_specs = (
        P(None, None, ("slab", "sub"), None),
        P(None, ("slab", "sub"), None),
        P(),
        P(None, ("slab", "sub"), None),
        P(("slab", "sub")),
        P(None, ("slab", "sub"), None),
    )
    out_specs = (P(None, None, ("slab", "sub"), None), P(None, ("slab", "sub"), None))
    return jax.shard_map(local, mesh=mesh, in_specs=in_specs, out_specs=out_specs, check_vma=False)
```

```python
import functools

import jax
import jax.numpy as jnp
import numpy as np
from jax import lax
from jax.experimental import pallas as pl
from jax.experimental.pallas import tpu as pltpu
from jax.sharding import PartitionSpec as P

MESH = pl.DeviceIdType.MESH
F32 = jnp.float32

POINTS = np.cos(np.pi * np.arange(8) / 7.0)


def derivative():
    endings = np.ones(8)
    endings[0] = endings[7] = 2.0
    weighted = endings * (-1.0) ** np.arange(8)
    spacing = POINTS[:, None] - POINTS[None, :] + np.eye(8)
    derive = weighted[:, None] / weighted[None, :] / spacing
    return derive - np.eye(8) * np.sum(derive, axis=1)[:, None]


D = derivative()
K = D.T @ D
COLUMN_SQ = np.sum(D * D, axis=0)
H = np.stack([(1.0 - POINTS) / 2.0, (1.0 + POINTS) / 2.0])


def half_tables(matrix):
    even = (matrix[:4, :4] + matrix[:4, :3:-1]) / 2.0
    odd = (matrix[:4, :4] - matrix[:4, :3:-1]) / 2.0
    return even.tolist(), odd.tolist()


D_EVEN, D_ODD = half_tables(D)
K_EVEN, K_ODD = half_tables(K)


def dot4(row, parts):
    total = row[0] * parts[0]
    for a in range(1, 4):
        total = total + row[a] * parts[a]
    return total


def split(x):
    return [x[a] + x[7 - a] for a in range(4)], [x[a] - x[7 - a] for a in range(4)]


def apply_d(even, odd, p):
    from_even, from_odd = dot4(D_EVEN[p], even), dot4(D_ODD[p], odd)
    return from_odd + from_even, from_odd - from_even


def apply_k(even, odd, p):
    from_even, from_odd = dot4(K_EVEN[p], even), dot4(K_ODD[p], odd)
    return from_even + from_odd, from_even - from_odd


def ring(n, d):
    return min(d, n - d)


def kernel(
    sizes, fields, heat, metric, diffusivity, flip, decay, s, fg, backs,
    f, q, met, dif, flp, dec, u, tt, dv, res, wgt, proj,
    face_l, face_r, got_l, got_r, pface_l, pface_r, pgot_l, pgot_r,
    near_out, near, mine, partner, rates, edge,
    y_stat, y_push, y_pre, x_stat, x_push, x_pre, z_all, z_back, z_push, z_pre,
    load_sem, face_send, face_recv, pface_send, pface_recv, near_send, near_recv,
    pair_sem, rate_sem, swap_sem, edge_send, edge_recv, push_send, push_recv, stat_send, stat_recv,
    stat_tail_send, stat_tail_recv, push_tail_send, push_tail_recv, both_sem, heard,
):
    nz, nx, ny = sizes
    chips_n = nx * ny
    sub_n = 2 * chips_n
    total = nz * sub_n
    z, sub = lax.axis_index("slab"), lax.axis_index("sub")
    core = lax.rem(sub, 2)
    chip = lax.div(sub, 2)
    cx, cy = lax.div(chip, ny), lax.rem(chip, ny)
    here = z * sub_n + sub
    at_start, at_end = here == 0, here == total - 1
    side = 2 * core - 1

    def at(position):
        position = lax.rem(position + total, total)
        return (lax.div(position, sub_n), lax.rem(position, sub_n))

    other_core = (z, sub - side)
    before, after = at(here - 1), at(here + 1)
    outer, outer_two, inner_two = at(here + side), at(here + 2 * side), at(here - 2 * side)
    chip_at = z * chips_n + chip
    more_before, more_after = chip_at > 0, chip_at < nz * chips_n - 1
    has_outer = jnp.where(core == 0, more_before, more_after)
    has_inner = jnp.where(core == 0, more_after, more_before)
    by_distance = lambda n: sorted(range(1, n), key=lambda d: -ring(n, d))
    y_order, x_order, z_order = by_distance(ny), by_distance(nx), by_distance(nz)

    def shift(dx, dy, dz):
        px, py = lax.rem(cx + dx + nx, nx), lax.rem(cy + dy + ny, ny)
        return (lax.rem(z + dz + nz, nz), (px * ny + py) * 2 + core)

    y_peers = [shift(0, d, 0) for d in y_order]
    x_peers = [shift(d, 0, 0) for d in x_order]
    z_peers = [shift(0, 0, d) for d in z_order]

    def remote(src, dst, send_sem, recv_sem, device):
        return pltpu.make_async_remote_copy(
            src_ref=src, dst_ref=dst, send_sem=send_sem, recv_sem=recv_sem,
            device_id=device, device_id_type=MESH,
        )

    def send(*args):
        copy = remote(*args)
        copy.start()
        return copy

    def when(condition, action):
        if condition is None:
            action()
        else:
            pl.when(condition)(action)

    class Exchange:
        def __init__(self, parts):
            self.parts = [(sent, got, remote(*args)) for sent, got, args in parts]

        def start(self):
            for sent, _, copy in self.parts:
                when(sent, copy.start)

        def wait(self):
            for sent, got, copy in self.parts:
                when(got, copy.wait_recv)
                when(sent, copy.wait_send)

    def wait_bytes(ref, sem):
        pltpu.make_async_copy(ref, ref, sem).wait()

    def offsets(n, wanted):
        return sorted({d % n for d in wanted} - {0})

    near_x = offsets(nx, (1, 2, 3))
    near_y = offsets(ny, (1, 2, -1, -2))
    near_z = offsets(nz, (1, 2, -1, -2))
    z_back[...] = jnp.zeros((nz, 2, 8, 128), F32)
    barrier = pltpu.get_barrier_semaphore()
    targets = [other_core] + [shift(d, 0, 0) for d in near_x]
    targets += [shift(0, d, 0) for d in near_y] + [shift(0, 0, d) for d in near_z]
    for condition, device in ((has_outer, outer), (has_inner, inner_two)):

        @pl.when(condition)
        def _():
            pl.semaphore_signal(barrier, inc=1, device_id=device, device_id_type=MESH)

    for device in targets:
        pl.semaphore_signal(barrier, inc=1, device_id=device, device_id_type=MESH)
    def load(src, dst, rows, k):
        return pltpu.make_async_copy(src.at[rows], dst.at[rows], load_sem.at[k])

    loads = [
        pltpu.make_async_copy(decay, dec, load_sem.at[0]),
        pltpu.make_async_copy(metric, met, load_sem.at[1]),
        pltpu.make_async_copy(flip, flp, load_sem.at[2]),
        pltpu.make_async_copy(diffusivity, dif, load_sem.at[3]),
    ]
    loads += [load(fields, f, pl.ds(512 * n, 512), 4 + n) for n in range(3)]
    ends_of = [512 * n + at_plane for n in (3, 4) for at_plane in (0, 448)]
    loads += [load(fields, f, pl.ds(spot, 64), 7 + k) for k, spot in enumerate(ends_of)]
    later = [load(fields, f, pl.ds(512 * n + 64, 384), 8 + n) for n in (3, 4)]
    later.append(pltpu.make_async_copy(heat, q, load_sem.at[13]))
    for copy in loads:
        copy.start()

    second = [shift(0, d, 0) for d in offsets(ny, (2, -2))] + [shift(0, 0, d) for d in offsets(nz, (2, -2))]
    third = [shift(0, 0, d) for d in offsets(nz, (4, -4))]

    def pass_word(k, devices):
        for device in devices:
            pl.semaphore_signal(heard.at[k], inc=1, device_id=device, device_id_type=MESH)

    for copy in loads:
        copy.wait()
    for copy in later:
        copy.start()

    row = lax.broadcasted_iota(jnp.int32, (8, 128), 0)
    zero = jnp.zeros((8, 128), F32)
    wall = jnp.where((row == 0) | (row == 7), 0.0, 1.0)
    turned = (zero + flp[0].astype(F32)) == 1.0
    m = [jnp.broadcast_to(met[d], (8, 128)) for d in range(3)]
    msq = [m[d] * m[d] for d in range(3)]

    def by_row(values):
        out = zero + float(values[7])
        for k in range(7):
            out = jnp.where(row == k, float(values[k]), out)
        return out

    def reverse(x):
        half = pltpu.roll(x, 4, 0)
        pairs = jnp.where(lax.rem(row, 4) < 2, pltpu.roll(half, 6, 0), pltpu.roll(half, 2, 0))
        return jnp.where(lax.rem(row, 2) == 0, pltpu.roll(pairs, 7, 0), pltpu.roll(pairs, 1, 0))

    def oriented(x):
        return jnp.where(turned, reverse(x), x)

    def tile(ref, base):
        return ref.at[pl.ds(pl.multiple_of(base, 8), 8), :]

    def strided(ref, base, k):
        return ref[pl.ds(base + k, 8, stride=8), :]

    def start_velocity(i):
        def line(j, carry):
            at_row = i * 64 + j * 8
            x = [tile(f, n * 512 + at_row)[...] for n in range(5)]
            lifting = 0.015 * x[3] - 0.0125 - 0.0125 * jnp.tanh(0.5 * x[4])
            for n in range(3):
                tile(s, n * 512 + at_row)[...] = x[n] + lifting if n == 1 else x[n]
                tile(u, n * 512 + at_row)[...] = 0.01 * m[n] * x[n]
            return carry

        lax.fori_loop(0, 8, line, 0, unroll=4)

    def start_scalars(i):
        def line(j, carry):
            at_row = i * 64 + j * 8
            warmth, bubbles = tile(f, 1536 + at_row)[...], tile(f, 2048 + at_row)[...]
            warm, share = 0.05 + 0.025 * jnp.tanh(warmth), 0.5 - 0.5 * jnp.tanh(0.5 * bubbles)
            heating = tile(q, at_row)[...] * warm * share
            tile(s, 1536 + at_row)[...] = warmth + heating
            tile(s, 2048 + at_row)[...] = bubbles + 0.2 * heating
            return carry

        lax.fori_loop(0, 8, line, 0, unroll=4)

    def step_planes(n, planes):
        rate = dif[n]
        c1, c2 = rate * msq[1], rate * msq[2]
        for slot, i in enumerate(planes):
            at_row = i * 64
            even, odd = split([strided(f, n * 512 + at_row, k) for k in range(8)])
            for p in range(4):
                slopes, bends = apply_d(even, odd, p), apply_k(even, odd, p)
                for k, slope, bend in zip((p, 7 - p), slopes, bends):
                    spot = 64 * slot + 8 * k
                    tt[spot : spot + 8, :] = strided(u, 1024 + at_row, k) * slope + c2 * bend
        for slot, i in enumerate(planes):
            at_row = i * 64
            base = n * 512 + at_row
            even, odd = split([tile(f, base + 8 * j)[...] for j in range(8)])
            for p in range(4):
                slopes, bends = apply_d(even, odd, p), apply_k(even, odd, p)
                for j, slope, bend in zip((p, 7 - p), slopes, bends):
                    gone = tile(u, 512 + at_row + 8 * j)[...] * slope + c1 * bend
                    gone = gone + strided(tt, 64 * slot, j)
                    tile(s, base + 8 * j)[...] = tile(s, base + 8 * j)[...] - gone

    def step_lines(n, pairs):
        c0 = dif[n] * msq[0]
        keep = jnp.where(zero + (n < 3).astype(F32) > 0.5, wall, 1.0)

        def line(j, carry):
            base = n * 512 + j * 8
            even, odd = split([tile(f, base + 64 * i)[...] for i in range(8)])
            for p in pairs:
                slopes, bends = apply_d(even, odd, p), apply_k(even, odd, p)
                for i, slope, bend in zip((p, 7 - p), slopes, bends):
                    gone = tile(u, i * 64 + j * 8)[...] * slope + c0 * bend
                    tile(s, base + 64 * i)[...] = keep * (tile(s, base + 64 * i)[...] - gone)
            return carry

        lax.fori_loop(0, 8, line, 0, unroll=4)

    def join_span(ref, base):
        low, high = tile(ref, base), tile(ref, base + 56)
        shared = 0.5 * (low[...] + pltpu.roll(high[...], 1, 1))
        low[...] = shared
        high[...] = pltpu.roll(shared, 127, 1)

    def stage_faces(n):
        for j in range(8):
            spot = n * 64 + 8 * j
            tile(face_l, spot)[...] = oriented(tile(s, n * 512 + 8 * j)[...])
            tile(face_r, spot)[...] = tile(s, n * 512 + 448 + 8 * j)[...]

    def each(low, high, body, unroll=1):
        def run(n, carry):
            body(n)
            return carry

        lax.fori_loop(low, high, run, 0, unroll=unroll)

    near_out[0:8, :] = dec[...]
    near_out[8:16, :] = zero + flp[0].astype(F32)

    for i in (0, 7):
        start_velocity(i)

    def velocity_faces(n):
        step_planes(n, (0, 7))
        step_lines(n, (0,))
        for i in (0, 7):
            join_span(s, n * 512 + i * 64)
        stage_faces(n)

    each(0, 3, velocity_faces)

    pl.semaphore_wait(barrier, len(targets) + 2 * has_outer.astype(jnp.int32))
    def chain_exchange(left, right, from_left, from_right, sems, k):
        ahead, behind = jnp.logical_not(at_end), jnp.logical_not(at_start)
        return Exchange([
            (behind, ahead, (left, from_right, sems[0].at[k], sems[1].at[k], before)),
            (ahead, behind, (right, from_left, sems[0].at[k + 1], sems[1].at[k + 1], after)),
        ])

    def face_exchange(n, count, k):
        rows = pl.ds(n * 64, count * 64)
        return chain_exchange(
            face_l.at[rows], face_r.at[rows], got_l.at[rows], got_r.at[rows], (face_send, face_recv), k
        )

    pass_word(0, second)
    nears = Exchange([
        (None, None, (near_out, near.at[0], near_send.at[0], near_recv.at[0], other_core)),
        (has_outer, has_outer, (near_out, near.at[1], near_send.at[1], near_recv.at[1], outer)),
        (has_outer, has_inner, (near_out, near.at[2], near_send.at[2], near_recv.at[2], outer_two)),
    ])
    nears.start()
    for condition, k in ((has_outer, 1), (has_inner, 2)):

        @pl.when(jnp.logical_not(condition))
        def _():
            near[k] = jnp.zeros((16, 128), F32)

    for n in range(3):
        face_exchange(n, 1, 2 * n).start()

    for copy in later:
        copy.wait()
    each(1, 7, start_velocity)

    def velocity_rest(n):
        def planes(t, carry):
            step_planes(n, (1 + 2 * t, 2 + 2 * t))
            return carry

        lax.fori_loop(0, 3, planes, 0)
        step_lines(n, (1, 2, 3))
        for i in range(1, 7):
            join_span(s, n * 512 + i * 64)

    each(0, 2, velocity_rest)
    pl.semaphore_wait(heard.at[0], len(second))
    pass_word(1, third)
    rates[core, cy + 1] = dec[...]
    for device in y_peers:
        send(dec, rates.at[core, cy + 1], rate_sem.at[0], rate_sem.at[1], device)
    each(2, 3, velocity_rest)

    across = msq[2] * by_row(COLUMN_SQ) + 1.0
    for a in range(4):
        for b in range(4):
            under = across + (float(COLUMN_SQ[a]) * msq[0] + float(COLUMN_SQ[b]) * msq[1])
            wgt[8 * (4 * a + b) : 8 * (4 * a + b) + 8, :] = 0.5 / under

    nears.wait()
    own_a, partner_a, outer_a, far_a = dec[...], near[0, 0:8, :], near[1, 0:8, :], near[2, 0:8, :]
    first_core = zero + core.astype(F32) < 0.5
    not_start = 1.0 - at_start.astype(F32)
    not_end = 1.0 - at_end.astype(F32)
    a_0, a_1 = jnp.where(first_core, own_a, partner_a), jnp.where(first_core, partner_a, own_a)
    a_m, a_p = jnp.where(first_core, outer_a, far_a), jnp.where(first_core, far_a, outer_a)
    chip_first = (z * chips_n + chip == 0).astype(F32)
    chip_last = (z * chips_n + chip == nz * chips_n - 1).astype(F32)

    def root(a):
        return jnp.sqrt((1.0 - a) * (1.0 + a))

    s_0, s_1 = root(a_0), root(a_1)
    s_m, s_p = (1.0 - chip_first) * root(a_m), (1.0 - chip_last) * root(a_p)
    a_m, a_p = (1.0 - chip_first) * a_m, (1.0 - chip_last) * a_p

    edge[0] = a_m
    edge[1] = a_p
    ends = ((cy == 0, 0, (1, 0)), (cy == ny - 1, 1, (0, ny + 1)))
    for is_end, k, place in ends:

        @pl.when(is_end)
        def _():
            rates[place] = edge[k]
            for device in y_peers:
                send(edge.at[k], rates.at[place], edge_send.at[k], edge_recv.at[k], device)

    ends_last = row < 4
    A_0, A_1 = jnp.where(ends_last, a_0, a_1), jnp.where(ends_last, a_1, a_p)
    R_0, R_1 = jnp.where(ends_last, a_m, a_0), jnp.where(ends_last, a_0, a_1)
    C_1 = jnp.where(ends_last, a_0 * s_1 * a_1, s_1)
    s_own = jnp.where(first_core, s_0, s_1)
    a_before, s_before = jnp.where(first_core, a_m, a_0), jnp.where(first_core, s_m, s_0)
    a_after, s_after = jnp.where(first_core, a_1, a_p), jnp.where(first_core, s_1, s_p)
    k_1 = jnp.where(ends_last, s_own, a_after * s_own)
    k_2 = jnp.where(ends_last, own_a * s_before, s_after)
    k_3 = jnp.where(ends_last, a_before * s_own * s_own, s_own * s_own)
    k_4 = jnp.where(ends_last, a_before * s_own * k_2 + s_before * s_before, 0.0)
    flip_after = jnp.where(first_core, near[0, 8:16, :], near[1, 8:16, :]) == 1.0

    for n in range(3):
        face_exchange(n, 1, 2 * n).wait()
    start_mask, end_mask = zero + not_start > 0.5, zero + not_end > 0.5

    def join_chain(n):
        for j in range(8):
            spot = n * 64 + 8 * j
            low, high = tile(s, n * 512 + 8 * j), tile(s, n * 512 + 448 + 8 * j)
            low[...] = jnp.where(start_mask, 0.5 * (low[...] + oriented(tile(got_l, spot)[...])), low[...])
            high[...] = jnp.where(end_mask, 0.5 * (high[...] + tile(got_r, spot)[...]), high[...])

    each(0, 3, join_chain)

    def divergence_planes(t):
        for slot in range(2):
            at_row = (2 * t + slot) * 64
            even, odd = split([strided(s, 1024 + at_row, k) for k in range(8)])
            for p in range(4):
                for k, slope in zip((p, 7 - p), apply_d(even, odd, p)):
                    spot = 64 * slot + 8 * k
                    tt[spot : spot + 8, :] = m[2] * slope
        for slot in range(2):
            at_row = (2 * t + slot) * 64
            even, odd = split([tile(s, 512 + at_row + 8 * j)[...] for j in range(8)])
            for p in range(4):
                for j, slope in zip((p, 7 - p), apply_d(even, odd, p)):
                    tile(dv, at_row + 8 * j)[...] = m[1] * slope + strided(tt, 64 * slot, j)

    each(0, 4, divergence_planes, 2)

    def guess_line(j):
        even, odd = split([tile(s, 64 * i + 8 * j)[...] for i in range(8)])
        nearer = jnp.minimum(j, 7 - j)
        for p in range(4):
            weight = tile(wgt, 8 * (4 * p + nearer))[...]
            for i, slope in zip((p, 7 - p), apply_d(even, odd, p)):
                spot = tile(dv, 64 * i + 8 * j)
                whole = spot[...] + m[0] * slope
                spot[...] = whole
                tile(fg, 64 * i + 8 * j)[...] = weight * whole

    each(0, 8, guess_line, 4)

    def residual_planes(t):
        for slot in range(2):
            at_row = (2 * t + slot) * 64
            even, odd = split([strided(fg, at_row, k) for k in range(8)])
            for p in range(4):
                for k, bend in zip((p, 7 - p), apply_k(even, odd, p)):
                    spot = 64 * slot + 8 * k
                    tt[spot : spot + 8, :] = msq[2] * bend
        for slot in range(2):
            at_row = (2 * t + slot) * 64
            even, odd = split([tile(fg, at_row + 8 * j)[...] for j in range(8)])
            for p in range(4):
                for j, bend in zip((p, 7 - p), apply_k(even, odd, p)):
                    at_j = at_row + 8 * j
                    gone = tile(fg, at_j)[...] + msq[1] * bend + strided(tt, 64 * slot, j)
                    tile(res, at_j)[...] = tile(dv, at_j)[...] - gone

    each(0, 4, residual_planes, 2)

    def project_line(j):
        even, odd = split([tile(fg, 64 * i + 8 * j)[...] for i in range(8)])
        left = [None] * 8
        for p in range(4):
            for i, bend in zip((p, 7 - p), apply_k(even, odd, p)):
                left[i] = tile(res, 64 * i + 8 * j)[...] - msq[0] * bend
        low = high = None
        for i in range(1, 7):
            low = float(H[0, i]) * left[i] + (0.0 if low is None else low)
            high = float(H[1, i]) * left[i] + (0.0 if high is None else high)
        for n, part in enumerate((low, high, left[7], left[0])):
            tile(proj, n * 64 + 8 * j)[...] = part

    each(0, 8, project_line, 8)

    gap = [by_row(H[0]), by_row(H[1])]
    sums = []
    for n in range(4):
        x = [proj[n * 64 + 8 * j : n * 64 + 8 * j + 8, :] for j in range(8)]
        shared = 0.5 * (x[0] + pltpu.roll(x[7], 1, 1))
        x[0], x[7] = shared, pltpu.roll(shared, 127, 1)
        modes = []
        for b in range(2):
            part = None
            for j in range(8):
                if H[b, j] != 0.0:
                    part = float(H[b, j]) * x[j] + (0.0 if part is None else part)
            for e in range(2):
                modes.append(jnp.sum(part * gap[e], axis=0, keepdims=True) * (1.0 / 64.0))
        sums.append(modes)

    def rows_of(values):
        out = zero
        for k, value in enumerate(values):
            out = jnp.where(row == k, value, out)
        return out

    inside = rows_of(sums[0] + sums[1])
    on_face = rows_of(sums[2] + sums[3])
    across_face = rows_of(sums[3] + sums[2])
    swapped = rows_of([part[e] for part in (sums[3], sums[2]) for e in (1, 0, 3, 2)])
    swap = jnp.where(ends_last, turned.astype(F32), flip_after.astype(F32)) > 0.5
    pushed = 0.5 * jnp.where(swap, swapped, across_face)
    own_share = jnp.where(ends_last, 1.0 - 0.5 * not_end, 1.0 - 0.5 * not_start)
    rhs = inside + own_share * on_face

    b_own = k_1 * rhs + k_2 * pushed
    d_own = k_3 * rhs + k_4 * pushed
    mine[0] = b_own
    mine[1] = d_own
    pair = send(mine, partner, pair_sem.at[0], pair_sem.at[1], other_core)
    pair.wait()
    B_0, D_0 = jnp.where(first_core, b_own, partner[0]), jnp.where(first_core, d_own, partner[1])
    B_1, D_1 = jnp.where(first_core, partner[0], b_own), jnp.where(first_core, partner[1], d_own)
    y_push[cy, 0] = A_1 * B_0 + B_1
    y_push[cy, 1] = D_0 + R_0 * (C_1 * B_0 + D_1)

    def spread(ref, place, k, sems, devices):
        for device in devices:
            send(ref.at[place], ref.at[place], sems[0].at[k], sems[1].at[k], device)

    def spread_ended(ref, k, sem, devices):
        wait_bytes(ref.at[0 : len(devices)], sem.at[k])

    pushes, stats = (push_send, push_recv), (stat_send, stat_recv)
    def spread_z(ref, first, sems, k, tail_sems):
        rest = pl.ds(first, ref.shape[1] - first)
        for d, device in zip(z_order, z_peers):
            head = ref.at[z, pl.ds(0, first)]
            send(head, head, sems[0].at[k], sems[1].at[k], device)

            @pl.when(z + d >= nz)
            def _():
                tail = ref.at[z, rest]
                send(tail, tail, tail_sems[0].at[d], tail_sems[1].at[z], device)

    def spread_z_got(ref, first, sem, k, tail_sem):
        rest = pl.ds(first, ref.shape[1] - first)
        wait_bytes(ref.at[0 : nz - 1, pl.ds(0, first)], sem.at[k])
        for n in range(1, nz):

            @pl.when(z < n)
            def _():
                wait_bytes(ref.at[n, rest], tail_sem.at[n])

    def spread_z_left(ref, first, sem, k, tail_sem):
        rest = pl.ds(first, ref.shape[1] - first)
        wait_bytes(ref.at[0 : nz - 1, pl.ds(0, first)], sem.at[k])
        for d in range(1, nz):

            @pl.when(z + d >= nz)
            def _():
                wait_bytes(ref.at[z, rest], tail_sem.at[d])

    z_push_tail = (push_tail_send, push_tail_recv)
    spread(y_push, cy, 0, pushes, y_peers)

    wait_bytes(rates.at[core, pl.ds(1, ny - 1)], rate_sem.at[1])
    half = rates.at[core, pl.ds(1, ny)]
    swap_halves = send(half, half, swap_sem.at[0], swap_sem.at[1], other_core)
    for is_end, k, place in ends:

        @pl.when(jnp.logical_not(is_end))
        def _():
            wait_bytes(rates.at[place], edge_recv.at[k])

    swap_halves.wait()

    roots = [[root(rates[c, n + 1]) for n in range(ny)] for c in range(2)]
    for n in range(ny):
        e_m, e_0 = rates[1, n], rates[0, n + 1]
        e_1, e_p = rates[1, n + 1], rates[0, n + 2]
        both, lead = e_0 * e_1, e_m * e_0
        mixed = roots[0][n] + both * roots[1][n]
        y_stat[n, 0] = jnp.where(ends_last, both, e_1 * e_p)
        y_stat[n, 1] = jnp.where(ends_last, lead, both)
        y_stat[n, 2] = jnp.where(ends_last, lead * mixed, mixed)

    ones = zero + 1.0

    def combine_stat(stat, pre, count):
        up = ones
        for n in range(count):
            pre[n, 0] = up
            up = stat[n, 0] * up
        down, mixed = ones, zero
        for n in range(count - 1, -1, -1):
            pre[n, 1] = down
            pre[n, 2] = mixed
            mixed = stat[n, 1] * mixed + stat[n, 2] * pre[n, 0]
            down = stat[n, 1] * down
        return up, down, mixed

    def combine_push(stat, push, pre, count):
        up = zero
        for n in range(count):
            pre[n, 3] = up
            up = stat[n, 0] * up + push[n, 0]
        down = zero
        for n in range(count - 1, -1, -1):
            pre[n, 4] = down
            down = stat[n, 1] * down + (stat[n, 2] * pre[n, 3] + push[n, 1])
        return up, down

    def set_stat(ref, place, values):
        for k, value in enumerate(values):
            ref[place, k] = value

    set_stat(x_stat, cx, combine_stat(y_stat, y_pre, ny))
    spread(x_stat, cx, 0, stats, x_peers)

    each(0, 8, start_scalars)

    def scalars(n):
        def planes(t, carry):
            step_planes(n, (2 * t, 2 * t + 1))
            return carry

        lax.fori_loop(0, 4, planes, 0)
        step_lines(n, (0, 1, 2, 3))
        for i in range(8):
            join_span(s, n * 512 + i * 64)
        stage_faces(n)

    each(3, 5, scalars)
    for i in range(8):
        join_span(fg, 64 * i)
    for j in range(8):
        tile(pface_l, 8 * j)[...] = oriented(tile(fg, 8 * j)[...])
        tile(pface_r, 8 * j)[...] = tile(fg, 448 + 8 * j)[...]

    spread_ended(y_push, 0, push_recv, y_peers)
    set_stat(x_push, cx, combine_push(y_stat, y_push, y_pre, ny))
    spread(x_push, cx, 1, pushes, x_peers)
    pl.semaphore_wait(heard.at[1], len(third)) if third else None
    spread_ended(x_stat, 0, stat_recv, x_peers)
    slab_a, slab_r, slab_c = combine_stat(x_stat, x_pre, nx)

    @pl.when(core == 0)
    def _():
        z_all[z] = slab_a
        for device in z_peers:
            send(z_all.at[z], z_all.at[z], stat_send.at[1], stat_recv.at[1], device)

    @pl.when(core == 1)
    def _():
        z_back[z, 0] = slab_r
        z_back[z, 1] = slab_c

    for d, device in zip(z_order, z_peers):

        @pl.when((core == 1) & (z + d >= nz))
        def _():
            send(z_back.at[z], z_back.at[z], stat_tail_send.at[d], stat_tail_recv.at[z], device)


    guess_exchange = chain_exchange(pface_l, pface_r, pgot_l, pgot_r, (pface_send, pface_recv), 0)
    guess_exchange.start()
    face_exchange(3, 2, 6).start()
    spread_ended(x_push, 1, push_recv, x_peers)
    set_stat(z_push, z, combine_push(x_stat, x_push, x_pre, nx))
    spread_z(z_push, 1, pushes, 2, z_push_tail)
    wait_bytes(rates.at[core, pl.ds(1, ny - 1)], rate_sem.at[0])
    spread_ended(y_push, 0, push_send, y_peers)
    spread_ended(x_stat, 0, stat_send, x_peers)
    spread_ended(x_push, 1, push_send, x_peers)
    for is_end, k, place in ends:

        @pl.when(is_end)
        def _():
            wait_bytes(rates.at[0, pl.ds(1, ny - 1)], edge_send.at[k])

    all_share = remote(z_all, z_all, both_sem.at[0], both_sem.at[1], other_core)
    back_share = remote(z_back, z_back, both_sem.at[2], both_sem.at[3], other_core)
    for n in range(1, nz):

        @pl.when((core == 1) & (z < n))
        def _():
            wait_bytes(z_back.at[n], stat_tail_recv.at[n])

    @pl.when(core == 1)
    def _():
        back_share.start()

    @pl.when(core == 0)
    def _():
        wait_bytes(z_all.at[0 : nz - 1], stat_recv.at[1])
        all_share.start()

    guess_exchange.wait()
    for j in range(8):
        low, high = tile(fg, 8 * j), tile(fg, 448 + 8 * j)
        low[...] = jnp.where(start_mask, 0.5 * (low[...] + oriented(tile(pgot_l, 8 * j)[...])), low[...])
        high[...] = jnp.where(end_mask, 0.5 * (high[...] + tile(pgot_r, 8 * j)[...]), high[...])
    face_exchange(3, 2, 6).wait()
    each(3, 5, join_chain)


    @pl.when(core == 1)
    def _():
        all_share.wait_recv()
        back_share.wait_send()

    @pl.when(core == 0)
    def _():
        back_share.wait_recv()
        all_share.wait_send()

    spread_z_got(z_push, 1, push_recv, 2, push_tail_recv)

    up = zero
    for n in range(nz):
        z_pre[n, 3] = up
        up = z_all[n] * up + z_push[n, 0]
    down = zero
    for n in range(nz - 1, -1, -1):
        further = z_back[n, 0] * down + (z_back[n, 1] * z_pre[n, 3] + z_push[n, 1])
        down = jnp.where(zero + (n > z).astype(F32) > 0.5, further, zero)
        z_pre[n, 4] = down
    up = z_pre[z, 3]
    down = z_pre[lax.rem(z + 1, nz), 4]
    down = jnp.where(zero + (z + 1 < nz).astype(F32) > 0.5, down, zero)
    for pre, place in ((x_pre, cx), (y_pre, cy)):
        down = pre[place, 4] + pre[place, 1] * down + pre[place, 2] * up
        up = pre[place, 3] + pre[place, 0] * up
    chip_up, chip_down = up, down
    middle = A_0 * chip_up + B_0
    up = jnp.where(first_core, chip_up, middle)
    down = jnp.where(first_core, R_1 * chip_down + C_1 * middle + D_1, chip_down)
    back = jnp.where(
        ends_last, down + s_own * (own_a * up + b_own), own_a * down + s_own * (up + s_own * rhs)
    )

    backs[...] = back

    @pl.when(core == 0)
    def _():
        wait_bytes(z_all.at[0 : nz - 1], stat_send.at[1])

    for d in range(1, nz):

        @pl.when((core == 1) & (z + d >= nz))
        def _():
            wait_bytes(z_back.at[z], stat_tail_send.at[d])

    spread_z_left(z_push, 1, push_send, 2, push_tail_send)


def finish(adv, guess, back, adv_out, prs_out, fg, sem):
    move = pltpu.make_async_copy(adv, adv_out, sem.at[0])
    move.start()
    row = lax.broadcasted_iota(jnp.int32, (8, 128), 0)
    gap = []
    for b in range(2):
        values = jnp.full((8, 128), float(H[b, 7]), F32)
        for k in range(7):
            values = jnp.where(row == k, float(H[b, k]), values)
        gap.append(values)
    modes = [jnp.broadcast_to(back[k : k + 1, :], (8, 128)) for k in range(8)]
    edges = [gap[0] * modes[2 * k] + gap[1] * modes[2 * k + 1] for k in range(4)]
    for j in range(8):
        rims = [float(H[0, j]) * edges[2 * a] + float(H[1, j]) * edges[2 * a + 1] for a in range(2)]
        for i in range(8):
            at_ij = 64 * i + 8 * j
            guessed = guess[at_ij : at_ij + 8, :]
            fg[at_ij : at_ij + 8, :] = guessed + float(H[0, i]) * rims[0] + float(H[1, i]) * rims[1]
    out = pltpu.make_async_copy(fg, prs_out, sem.at[1])
    out.start()
    move.wait()
    out.wait()


def solution(mesh):
    nz, sub_n = mesh.shape["slab"], mesh.shape["sub"]
    nx = 2 if sub_n == 8 else 4
    ny = sub_n // (2 * nx)
    vmem = lambda *shape: pltpu.VMEM(shape, F32)
    dma = lambda n: pltpu.SemaphoreType.DMA((n,))
    anywhere = pl.BlockSpec(memory_space=pl.ANY)
    inside = pl.BlockSpec(memory_space=pltpu.VMEM)

    def local(fields, metric, diffusivity, joule_heat, face_flip, coarse_decay):
        fields_shape = jax.ShapeDtypeStruct((2560, 128), F32)
        node_shape = jax.ShapeDtypeStruct((512, 128), F32)
        mode_shape = jax.ShapeDtypeStruct((8, 128), F32)
        advanced, guess, back = pl.pallas_call(
            functools.partial(kernel, (nz, nx, ny)),
            name="step",
            out_shape=(pltpu.VMEM((2560, 128), F32), pltpu.VMEM((512, 128), F32), pltpu.VMEM((8, 128), F32)),
            in_specs=[anywhere] * 6,
            out_specs=(inside, inside, inside),
            scratch_shapes=[
                vmem(2560, 128),
                vmem(512, 128),
                vmem(3, 1, 128),
                pltpu.SMEM((5,), F32),
                pltpu.SMEM((1,), jnp.int32),
                vmem(8, 128),
                vmem(1536, 128),
                vmem(128, 128),
                vmem(512, 128),
                vmem(512, 128),
                vmem(128, 128),
                vmem(256, 128),
                vmem(320, 128),
                vmem(320, 128),
                vmem(320, 128),
                vmem(320, 128),
                vmem(64, 128),
                vmem(64, 128),
                vmem(64, 128),
                vmem(64, 128),
                vmem(16, 128),
                vmem(3, 16, 128),
                vmem(2, 8, 128),
                vmem(2, 8, 128),
                vmem(2, ny + 2, 8, 128),
                vmem(2, 8, 128),
                vmem(ny, 3, 8, 128), vmem(ny, 2, 8, 128), vmem(ny, 5, 8, 128),
                vmem(nx, 3, 8, 128), vmem(nx, 2, 8, 128), vmem(nx, 5, 8, 128),
                vmem(nz, 8, 128), vmem(nz, 2, 8, 128), vmem(nz, 2, 8, 128), vmem(nz, 5, 8, 128),
                dma(14), dma(8), dma(8), dma(2), dma(2), dma(3), dma(3),
                dma(2), dma(2), dma(2), dma(2), dma(2), dma(3), dma(3), dma(2), dma(2),
                dma(nz), dma(nz), dma(nz), dma(nz), dma(4),
                pltpu.SemaphoreType.REGULAR((2,)),
            ],
            compiler_params=pltpu.CompilerParams(
                collective_id=0, has_side_effects=True, vmem_limit_bytes=60 * 1024 * 1024
            ),
        )(
            fields.reshape(2560, 128), joule_heat.reshape(512, 128), metric, diffusivity,
            face_flip, coarse_decay.reshape(8, 128),
        )
        advanced, pressure = pl.pallas_call(
            finish,
            name="finish",
            out_shape=(fields_shape, node_shape),
            in_specs=[inside] * 3,
            out_specs=(anywhere, anywhere),
            scratch_shapes=[vmem(512, 128), dma(2)],
            compiler_params=pltpu.CompilerParams(vmem_limit_bytes=16 * 1024 * 1024),
        )(advanced, guess, back)
        return advanced.reshape(5, 512, 1, 128), pressure.reshape(512, 1, 128)

    in_specs = (
        P(None, None, ("slab", "sub"), None),
        P(None, ("slab", "sub"), None),
        P(),
        P(None, ("slab", "sub"), None),
        P(("slab", "sub")),
        P(None, ("slab", "sub"), None),
    )
    out_specs = (P(None, None, ("slab", "sub"), None), P(None, ("slab", "sub"), None))
    return jax.shard_map(local, mesh=mesh, in_specs=in_specs, out_specs=out_specs, check_vma=False)
```
